32 devices in a mesh: rows: 4 (over x, core), seq: 8 (over z, y).
Axes of the slice: x: 2, y: 2, z: 4, core: 2. Of those that a mesh axis runs over, the one named last changes fastest.
Arguments:
- inputs: bfloat16 [8, 1024, 2048], P('rows', 'seq'), may hold values from -6 to 6
- cotangent: bfloat16 [8, 1024, 2048], P('rows', 'seq'), may hold values from -6 to 6
- positions: int32 [8, 1024], P('rows', 'seq'), may hold values from 0 to 4095, as said below
- segment_ids: int32 [8, 1024], P('rows', 'seq'), may hold values from 0 to 3, as said below
- w_query: bfloat16 [2048, 1280], P(('rows', 'seq')), may hold values from -0.125 to 0.125
- w_key: bfloat16 [2048, 320], P(('rows', 'seq')), may hold values from -0.125 to 0.125
- w_value: bfloat16 [2048, 320], P(('rows', 'seq')), may hold values from -0.125 to 0.125
- w_out: bfloat16 [1280, 2048], P(('rows', 'seq')), may hold values from -0.625 to 0.625
- w_gate: bfloat16 [2048, 6656], P('seq', 'rows'), may hold values from -0.125 to 0.125
- w_up: bfloat16 [2048, 6656], P('seq', 'rows'), may hold values from -0.125 to 0.125
- w_down: bfloat16 [6656, 2048], P('rows', 'seq'), may hold values from -0.078125 to 0.078125
- gain_attn: bfloat16 [2048], P(('rows', 'seq')), may hold values from 0.5 to 1.5
- gain_query: bfloat16 [64], replicated, may hold values from 0.099609375 to 1.8984375
- gain_key: bfloat16 [64], replicated, may hold values from 0.099609375 to 1.8984375
- gain_ffn: bfloat16 [2048], P(('rows', 'seq')), may hold values from 0.5 to 1.5
Outputs:
- output: bfloat16 [8, 1024, 2048], P('rows', 'seq')
- grad_inputs: float32 [8, 1024, 2048], P('rows', 'seq')
- grad_query: float32 [2048, 1280], P(('rows', 'seq'))
- grad_key: float32 [2048, 320], P(('rows', 'seq'))
- grad_value: float32 [2048, 320], P(('rows', 'seq'))
- grad_out: float32 [1280, 2048], P(('rows', 'seq'))
- grad_gate: float32 [2048, 6656], P('seq', 'rows')
- grad_up: float32 [2048, 6656], P('seq', 'rows')
- grad_down: float32 [6656, 2048], P('rows', 'seq')
- grad_gain_attn: float32 [2048], P(('rows', 'seq'))
- grad_gain_query: float32 [64], replicated
- grad_gain_key: float32 [64], replicated
- grad_gain_ffn: float32 [2048], P(('rows', 'seq'))
The draws below stay inside these ranges and needn't reach their ends.
Inputs may be any that keep to these rules, and one draw needn't show every extreme that they name: `segment_ids`: within a packed row the ids never fall, start at 0, and every row holds exactly 4 documents of one token or more. Inside a document the positions rise by one from token to token; each document starts at its own position.
All inputs are finite; a program needn't handle non-finite values.
Results may differ from the reference program's by a relative error of at most 0.02.
Values may be sent and summed in bfloat16 or wider, within the bound.
No kernel may reach another device: no remote copies, remote signals or barrier semaphores. Data moves between devices by JAX's collectives and lax.ppermute only.
A program may use at most 256 MiB of HBM per device.

```python
import jax
import jax.numpy as jnp
from jax import lax

D = 2048
FF = 6656
HQ = 20
HK = 5
HD = 64
NSEG = 4
POS_MAX = 4095
ROWS = 8
ROW_LEN = 1024


def packed_layout(key):
    base_key = jax.random.fold_in(key, 17)
    row_keys = jax.random.split(base_key, ROWS)
    index_row = jnp.arange(ROW_LEN, dtype=jnp.int32)
    last_slot = jnp.arange(NSEG, dtype=jnp.int32)

    def one_row(row_key, row_number):
        cut_key, shift_key = jax.random.split(row_key)
        picked = jax.random.permutation(cut_key, ROW_LEN - 1)[:NSEG - 1].astype(jnp.int32) + 1
        cut_points = jnp.sort(picked)
        segment = jnp.sum((index_row[:, None] >= cut_points[None, :]).astype(jnp.int32), axis=1)
        bounds = jnp.concatenate([jnp.zeros((1,), jnp.int32), cut_points, jnp.full((1,), ROW_LEN, jnp.int32)])
        starts = bounds[:-1]
        lengths = bounds[1:] - starts
        shifts = jax.random.randint(shift_key, (NSEG,), 0, POS_MAX + 2 - lengths).astype(jnp.int32)
        first_row = row_number == 0
        shifts = jnp.where(first_row & (last_slot == NSEG - 1), POS_MAX + 1 - lengths, shifts)
        shifts = jnp.where(first_row & (last_slot == 0), 0, shifts)
        position_row = index_row - starts[segment] + shifts[segment]
        return (segment.astype(jnp.int32), position_row.astype(jnp.int32))
    return jax.vmap(one_row)(row_keys, jnp.arange(ROWS, dtype=jnp.int32))


def draw_positions(key, part):
    return packed_layout(key)[1]


def draw_segment_ids(key, part):
    return packed_layout(key)[0]


def block_levels(own_key, shape, cuts, smallest, top_value):
    def one(position, shards_of):
        steps = jax.random.uniform(jax.random.fold_in(jax.random.fold_in(own_key, 6), position), (shards_of,), jnp.float32, smallest / len(cuts), top_value / len(cuts))
        return jnp.repeat(jnp.exp(steps), shape[position] // shards_of).reshape((-1,) + (1,) * (len(shape) - position - 1))

    gain = one(*cuts[0])
    for cut in cuts[1:]:
        gain = gain * one(*cut)
    return gain


def normal_values(rng, shape, deviation, limit, pieces=(), held_as=jnp.bfloat16):
    values = deviation * jax.random.normal(rng, shape, jnp.float32)
    if pieces:
        values = values * block_levels(rng, shape, pieces, -0.22, 0.18)
    return jnp.clip(values, -limit, limit).astype(held_as)


def setup_inputs(seed: int = 0) -> dict:
    arg_keys = jax.random.split(jax.random.key(seed), 16)
    return {
        "inputs": normal_values(arg_keys[0], (ROWS, ROW_LEN, D), 1.0, 6.0, ((0, 4), (1, 8))),
        "cotangent": normal_values(arg_keys[1], (ROWS, ROW_LEN, D), 1.0, 6.0, ((0, 4), (1, 8))),
        "positions": draw_positions(jax.random.fold_in(arg_keys[15], 71), 0),
        "segment_ids": draw_segment_ids(jax.random.fold_in(arg_keys[15], 71), 0),
        "w_query": normal_values(arg_keys[4], (D, HQ * HD), D ** -0.5, 0.125, ((0, 32),)),
        "w_key": normal_values(arg_keys[5], (D, HK * HD), D ** -0.5, 0.125, ((0, 32),)),
        "w_value": normal_values(arg_keys[6], (D, HK * HD), D ** -0.5, 0.125, ((0, 32),)),
        "w_out": normal_values(arg_keys[7], (HQ * HD, D), (HQ * HD // 16) ** -0.5, 0.625, ((0, 32),)),
        "w_gate": normal_values(arg_keys[8], (D, FF), D ** -0.5, 0.125, ((0, 8), (1, 4))),
        "w_up": normal_values(arg_keys[9], (D, FF), D ** -0.5, 0.125, ((0, 8), (1, 4))),
        "w_down": normal_values(arg_keys[10], (FF, D), FF ** -0.5, 0.078125, ((0, 4), (1, 8))),
        "gain_attn": jnp.clip(1.0 + 0.1 * jax.random.normal(arg_keys[11], (D,), jnp.float32), 0.5, 1.5).astype(jnp.bfloat16),
        "gain_query": jnp.clip(1.0 + 0.18 * jax.random.normal(arg_keys[12], (HD,), jnp.float32), 0.099609375, 1.8984375).astype(jnp.bfloat16),
        "gain_key": jnp.clip(1.0 + 0.18 * jax.random.normal(arg_keys[13], (HD,), jnp.float32), 0.099609375, 1.8984375).astype(jnp.bfloat16),
        "gain_ffn": jnp.clip(1.0 + 0.1 * jax.random.normal(arg_keys[14], (D,), jnp.float32), 0.5, 1.5).astype(jnp.bfloat16),
    }


norm_eps = 1e-06
masked_score = -1e+30
highest = lax.Precision.HIGHEST

@jax.custom_vjp
def low(v):
    return lax.optimization_barrier(v.astype(jnp.bfloat16)).astype(jnp.float32)

@jax.custom_vjp
def low_back(v):
    return v

def low_keep(v):
    return (low(v), None)

def low_pass(kept, grad):
    return (grad,)

def back_keep(v):
    return (v, None)

def back_low(kept, grad):
    return (low(grad),)
low.defvjp(low_keep, low_pass)
low_back.defvjp(back_keep, back_low)

def rms_apply(values, gain_vec):
    row_scale = lax.rsqrt(lax.optimization_barrier(jnp.mean(values * values, axis=-1, keepdims=True)) + norm_eps)
    return values * row_scale * gain_vec

def rotary_tables(positions, head_dim):
    half_dim = head_dim // 2
    frequencies = 10000.0 ** (-2.0 * jnp.arange(half_dim).astype(jnp.float32) / head_dim)
    angles = positions.astype(jnp.float32)[..., None] * frequencies
    angles = jnp.concatenate([angles, angles], axis=-1)
    return (jnp.cos(angles), jnp.sin(angles))

def rotate(values, cosine, sine):
    half_dim = values.shape[-1] // 2
    turned = jnp.concatenate([-values[..., half_dim:], values[..., :half_dim]], axis=-1)
    return values * cosine + turned * sine

def matmul(left, right):
    return jnp.dot(left, right, precision=highest, preferred_element_type=jnp.float32)

def attend(query_rot, key_rot, value_low, segment_ids):
    span_len = min(512, ROW_LEN)
    blocks_per_row = ROW_LEN // span_len
    grouping = HQ // HK
    query_blocks = query_rot.reshape(ROWS * blocks_per_row, span_len, HK, grouping, HD)
    key_spots = jnp.arange(ROW_LEN, dtype=jnp.int32)

    def one_block(block_number):
        row_number = block_number // blocks_per_row
        block_start = block_number % blocks_per_row * span_len
        queries = lax.dynamic_index_in_dim(query_blocks, block_number, 0, keepdims=False)
        keys_row = lax.dynamic_index_in_dim(key_rot, row_number, 0, keepdims=False)
        values_row = lax.dynamic_index_in_dim(value_low, row_number, 0, keepdims=False)
        segs_row = lax.dynamic_index_in_dim(segment_ids, row_number, 0, keepdims=False)
        segs_query = lax.dynamic_slice_in_dim(segs_row, block_start, span_len)
        query_spots = block_start + jnp.arange(span_len, dtype=jnp.int32)
        scores = jnp.einsum('qhgd,khd->hgqk', queries, keys_row, precision=highest) * HD ** (-0.5)
        scores = low_back(scores)
        allowed = (key_spots[None, :] <= query_spots[:, None]) & (segs_query[:, None] == segs_row[None, :])
        scores = jnp.where(allowed, scores, masked_score)
        shifted = jnp.exp(scores - lax.optimization_barrier(jnp.max(scores, axis=-1, keepdims=True)))
        probs_low = low(shifted / lax.optimization_barrier(jnp.sum(shifted, axis=-1, keepdims=True)))
        mixed_out = jnp.einsum('hgqk,khd->qhgd', probs_low, values_row, precision=highest)
        return mixed_out.reshape(span_len, HQ * HD)
    blocks = lax.map(jax.checkpoint(one_block), jnp.arange(ROWS * blocks_per_row, dtype=jnp.int32))
    return blocks.reshape(ROWS * ROW_LEN, HQ * HD)

def forward(inputs, w_query, w_key, w_value, w_out, w_gate, w_up, w_down, gain_attn, gain_query, gain_key, gain_ffn, cosine, sine, segment_ids):
    flat_in = inputs.reshape(ROWS * ROW_LEN, D)
    normed = low(rms_apply(flat_in, gain_attn))
    query_pre = low_back(matmul(normed, w_query))
    key_pre = low_back(matmul(normed, w_key))
    value_low = low(low_back(matmul(normed, w_value)))
    query_rot = low(rotate(rms_apply(query_pre.reshape(ROWS * ROW_LEN, HQ, HD), gain_query), cosine, sine))
    key_rot = low(rotate(rms_apply(key_pre.reshape(ROWS * ROW_LEN, HK, HD), gain_key), cosine, sine))
    attended = attend(query_rot.reshape(ROWS, ROW_LEN, HQ, HD), key_rot.reshape(ROWS, ROW_LEN, HK, HD), value_low.reshape(ROWS, ROW_LEN, HK, HD), segment_ids)
    attended = low(low_back(attended))
    middle = flat_in + low_back(matmul(attended, w_out))
    ffn_in = low(rms_apply(middle, gain_ffn))
    gate_val = low_back(matmul(ffn_in, w_gate))
    up_val = low_back(matmul(ffn_in, w_up))
    hidden = low(jax.nn.silu(gate_val) * up_val)
    output = middle + low_back(matmul(hidden, w_down))
    return output.reshape(ROWS, ROW_LEN, D)

def reference(inputs, cotangent, positions, segment_ids, w_query, w_key, w_value, w_out, w_gate, w_up, w_down, gain_attn, gain_query, gain_key, gain_ffn):
    cosine, sine = rotary_tables(positions, HD)
    cosine = cosine.reshape(ROWS * ROW_LEN, 1, HD)
    sine = sine.reshape(ROWS * ROW_LEN, 1, HD)
    params = tuple((item.astype(jnp.float32) for item in (w_query, w_key, w_value, w_out, w_gate, w_up, w_down, gain_attn, gain_query, gain_key, gain_ffn)))

    def layer(inputs_f, *weights):
        return forward(inputs_f, *weights, cosine, sine, segment_ids)
    output, pullback = jax.vjp(layer, inputs.astype(jnp.float32), *params)
    grads = pullback(cotangent.astype(jnp.float32))
    return (output.astype(jnp.bfloat16), grads[0], grads[1], grads[2], grads[3], grads[4], grads[5], grads[6], grads[7], grads[8], grads[9], grads[10], grads[11])
```

```python
import jax
import jax.numpy as jnp
from jax import lax
from jax.sharding import PartitionSpec as P

norm_eps = 1e-06
masked_score = -1e30


def rms_apply(values, gain_vec):
    row_scale = lax.rsqrt(jnp.mean(values * values, axis=-1, keepdims=True) + norm_eps)
    return values * row_scale * gain_vec


def rms_back(values, gain_vec, grad_in):
    row_scale = lax.rsqrt(jnp.mean(values * values, axis=-1, keepdims=True) + norm_eps)
    weighted = grad_in * gain_vec
    inner_sum = jnp.sum(weighted * values, axis=-1, keepdims=True)
    grad_values = (
        row_scale * weighted
        - values * (row_scale * row_scale * row_scale) * inner_sum / values.shape[-1]
    )
    return (grad_values, grad_in * values * row_scale)


def rotary_tables(positions, head_dim):
    half_dim = head_dim // 2
    frequencies = 10000.0 ** (-2.0 * jnp.arange(half_dim).astype(jnp.float32) / head_dim)
    angles = positions.astype(jnp.float32)[..., None] * frequencies
    angles = jnp.concatenate([angles, angles], axis=-1)
    return (jnp.cos(angles), jnp.sin(angles))


def rotate(values, cosine, sine):
    half_dim = values.shape[-1] // 2
    turned = jnp.concatenate([-values[..., half_dim:], values[..., :half_dim]], axis=-1)
    return values * cosine + turned * sine


def rotate_back(grad_in, cosine, sine):
    half_dim = grad_in.shape[-1] // 2
    moved_part = grad_in * sine
    turned = jnp.concatenate([moved_part[..., half_dim:], -moved_part[..., :half_dim]], axis=-1)
    return grad_in * cosine + turned


def times_transposed(left, right):
    return lax.dot_general(
        left, right, (((1,), (1,)), ((), ())), preferred_element_type=jnp.float32
    )


def transposed_times(left, right):
    return lax.dot_general(
        left, right, (((0,), (0,)), ((), ())), preferred_element_type=jnp.float32
    )


def swap(values, axis_name, bit):
    count = lax.axis_size(axis_name)
    return lax.ppermute(values, axis_name, [(i, i ^ bit) for i in range(count)])


def ring(values, shift):
    count = lax.axis_size("seq")
    return lax.ppermute(values, "seq", [(i, (i + 2 * shift) % count) for i in range(count)])


def core_swap(values):
    return swap(values, "rows", 1)


def x_swap(values):
    return swap(values, "rows", 2)


def y_swap(values):
    return swap(values, "seq", 1)


def sum_all(values):
    for axis_name in ("rows", "seq"):
        bit = 1
        while bit < lax.axis_size(axis_name):
            values = values + swap(values, axis_name, bit)
            bit *= 2
    return values


def places():
    row_place = lax.axis_index("rows")
    seq_place = lax.axis_index("seq")
    return (row_place // 2, row_place % 2, seq_place // 2, seq_place % 2)


def in_order(first, other, bit, axis):
    return jnp.where(
        bit == 0, jnp.stack([first, other], axis=axis), jnp.stack([other, first], axis=axis)
    )


def ring_gather(values):
    pieces = [values]
    for _ in range(lax.axis_size("seq") // 2 - 1):
        pieces.append(ring(pieces[-1], -1))
    return pieces


def ring_scatter(pieces):
    count = len(pieces)
    moving = None
    for step in range(1, count):
        block = pieces[count - step]
        if moving is not None:
            block = (block.astype(jnp.float32) + moving.astype(jnp.float32)).astype(jnp.bfloat16)
        moving = ring(block, 1)
    return pieces[0].astype(jnp.float32) + moving.astype(jnp.float32)


def turn(values, start):
    count = values.shape[0]
    return lax.dynamic_slice_in_dim(jnp.concatenate([values, values], axis=0), start, count, 0)


def turn_columns(values, start, width):
    return lax.dynamic_slice_in_dim(
        jnp.concatenate([values, values], axis=1), start * width, values.shape[1], 1
    )


def gather_weights(values, x_first):
    x_at, core_at, z_at, y_at = places()
    planes = lax.axis_size("seq") // 2
    size, width = values.shape
    block = turn(jnp.stack(ring_gather(values)), (planes - z_at) % planes)
    if x_first:
        other = x_swap(block)
        block = in_order(block, other, x_at, 0)
        other = y_swap(block)
        block = in_order(block, other, y_at, 2)
    else:
        other = y_swap(block)
        block = in_order(block, other, y_at, 1)
        other = x_swap(block)
        block = in_order(block, other, x_at, 0)
    other = core_swap(block)
    return in_order(block, other, core_at, 1).reshape(8 * planes * size, width)


def pick(values, bit, axis):
    return (
        lax.dynamic_index_in_dim(values, bit, axis, keepdims=False),
        lax.dynamic_index_in_dim(values, 1 - bit, axis, keepdims=False),
    )


def add_low(left, right):
    return (left.astype(jnp.float32) + right.astype(jnp.float32)).astype(jnp.bfloat16)


def scatter_weights(values, x_first):
    x_at, core_at, z_at, y_at = places()
    planes = lax.axis_size("seq") // 2
    width = values.shape[1]
    block = values.reshape(2, 2, planes, 2, -1, width)
    keep, send = pick(block, core_at, 1)
    block = add_low(keep, core_swap(send.astype(jnp.bfloat16)))
    if x_first:
        keep, send = pick(block, x_at, 0)
        block = add_low(keep, x_swap(send))
        keep, send = pick(block, y_at, 1)
        block = add_low(keep, y_swap(send))
    else:
        keep, send = pick(block, y_at, 2)
        block = add_low(keep, y_swap(send))
        keep, send = pick(block, x_at, 0)
        block = add_low(keep, x_swap(send))
    block = turn(block, z_at)
    return ring_scatter([block[t] for t in range(planes)])


def gather_tokens(values):
    half = values.shape[1] // 2
    from_x = x_swap(values)
    from_y = y_swap(values)
    from_xy = jnp.concatenate([y_swap(from_x[:, :half]), x_swap(from_y[:, half:])], axis=1)
    blocks = [values, from_x, from_y, from_xy]
    return jnp.concatenate(blocks + [core_swap(block) for block in blocks], axis=0)


def scatter_tokens(values):
    count = values.shape[0] // 8
    half = values.shape[1] // 2
    near = values[: 4 * count]
    far = core_swap(values[4 * count :].astype(jnp.bfloat16))
    total = near.astype(jnp.float32) + far.astype(jnp.float32)
    own, to_x, to_y, to_xy = [total[i * count : (i + 1) * count] for i in range(4)]
    corner = to_xy.astype(jnp.bfloat16)
    via_x = x_swap(corner[:, :half]).astype(jnp.float32)
    via_y = y_swap(corner[:, half:]).astype(jnp.float32)
    to_y = jnp.concatenate([to_y[:, :half] + via_x, to_y[:, half:]], axis=1)
    to_x = jnp.concatenate([to_x[:, :half], to_x[:, half:] + via_y], axis=1)
    from_x = x_swap(to_x.astype(jnp.bfloat16)).astype(jnp.float32)
    from_y = y_swap(to_y.astype(jnp.bfloat16)).astype(jnp.float32)
    return own + from_x + from_y


def local(
    inputs,
    cotangent,
    positions,
    segment_ids,
    w_query,
    w_key,
    w_value,
    w_out,
    w_gate,
    w_up,
    w_down,
    gain_attn,
    gain_query,
    gain_key,
    gain_ffn,
):
    rows_here, seg_tok, feature_count = inputs.shape
    tokens_here = rows_here * seg_tok
    head_dim = gain_query.shape[0]
    heads_query = w_query.shape[1] // head_dim
    heads_kv = w_key.shape[1] // head_dim
    grouping = heads_query // heads_kv
    row_len = seg_tok * lax.axis_size("seq")
    key_block = min(512, row_len)
    block_total = row_len // key_block
    score_scale = head_dim ** (-0.5)
    seq_place = lax.axis_index("seq")
    x_at, core_at, z_at, y_at = places()
    planes = lax.axis_size("seq") // 2
    place = lax.axis_index("rows") * lax.axis_size("seq") + seq_place
    gain_size = gain_attn.shape[0]
    gains = jnp.zeros((2 * feature_count,), jnp.float32)
    gains = lax.dynamic_update_slice_in_dim(
        gains, gain_attn.astype(jnp.float32), place * gain_size, 0
    )
    gains = lax.dynamic_update_slice_in_dim(
        gains, gain_ffn.astype(jnp.float32), feature_count + place * gain_size, 0
    )
    gains = sum_all(gains.reshape(-1, 128)).reshape(-1)
    attn_gain_full = gains[:feature_count]
    ffn_gain_full = gains[feature_count:]
    width_q, width_k = w_query.shape[1], w_key.shape[1]
    qkv_here = jnp.concatenate([w_query, w_key, w_value], axis=1)
    qkv_cut = 1024
    qkv_full = jnp.concatenate(
        [
            gather_weights(qkv_here[:, :qkv_cut], True),
            gather_weights(qkv_here[:, qkv_cut:], False),
        ],
        axis=1,
    )
    out_cut = feature_count // 2
    out_full = jnp.concatenate(
        [gather_weights(w_out[:, :out_cut], True), gather_weights(w_out[:, out_cut:], False)],
        axis=1,
    )
    residual = inputs.astype(jnp.float32).reshape(tokens_here, feature_count)
    normed = rms_apply(residual, attn_gain_full).astype(jnp.bfloat16)
    qkv_pre = jnp.dot(normed, qkv_full, preferred_element_type=jnp.float32)
    query_pre = qkv_pre[:, :width_q]
    key_pre = qkv_pre[:, width_q : width_q + width_k]
    value_pre = qkv_pre[:, width_q + width_k :]
    cosine, sine = rotary_tables(positions.reshape(tokens_here), head_dim)
    cosine = cosine[:, None, :]
    sine = sine[:, None, :]
    query_heads = query_pre.reshape(tokens_here, heads_query, head_dim)
    key_heads = key_pre.reshape(tokens_here, heads_kv, head_dim)
    gain_q = gain_query.astype(jnp.float32)
    gain_k = gain_key.astype(jnp.float32)
    query_b = rotate(rms_apply(query_heads, gain_q), cosine, sine).astype(jnp.bfloat16)
    query_b = query_b.reshape(rows_here, seg_tok, heads_kv, grouping, head_dim)
    key_b = rotate(rms_apply(key_heads, gain_k), cosine, sine).astype(jnp.bfloat16)
    key_b = key_b.reshape(rows_here, seg_tok, heads_kv * head_dim)
    value_b = value_pre.astype(jnp.bfloat16).reshape(rows_here, seg_tok, heads_kv * head_dim)
    kv_width = 2 * heads_kv * head_dim
    kv_here = jnp.concatenate([key_b, value_b], axis=2)

    def gather_seq(values):
        pieces = ring_gather(values)
        pieces = [in_order(piece, y_swap(piece), y_at, 0) for piece in pieces]
        return turn(jnp.stack(pieces), (planes - z_at) % planes)

    def row_of(values):
        moved = jnp.moveaxis(values, 2, 0)
        return moved.reshape((rows_here, row_len) + values.shape[4:])

    kv_all = row_of(gather_seq(kv_here))
    keys_all = kv_all[..., : kv_width // 2]
    values_all = kv_all[..., kv_width // 2 :]
    seg_keys = row_of(gather_seq(segment_ids))
    seg_query = segment_ids.astype(jnp.float32)
    query_spots = seq_place * seg_tok + jnp.arange(seg_tok, dtype=jnp.int32)
    stat_shape = (rows_here, heads_kv, grouping, seg_tok)

    def block_keys(block_start):
        keys_blk = lax.dynamic_slice_in_dim(keys_all, block_start, key_block, 1)
        values_blk = lax.dynamic_slice_in_dim(values_all, block_start, key_block, 1)
        shape_blk = (rows_here, key_block, heads_kv, head_dim)
        return (keys_blk.reshape(shape_blk), values_blk.reshape(shape_blk))

    def block_scores(block_start, keys_blk):
        scores = (
            jnp.einsum("rqhgd,rkhd->rhgqk", query_b, keys_blk, preferred_element_type=jnp.float32)
            * score_scale
        )
        key_spots = block_start + jnp.arange(key_block, dtype=jnp.int32)
        seg_blk = lax.dynamic_slice_in_dim(seg_keys, block_start, key_block, 1).astype(jnp.float32)
        allowed = (key_spots[None, None, :] <= query_spots[None, :, None]) & (
            seg_blk[:, None, :] == seg_query[:, :, None]
        )
        return jnp.where(allowed[:, None, None], scores, masked_score)

    def stats_step(block_index, state_in):
        running_max, running_sum = state_in
        block_start = block_index * key_block
        keys_blk, values_blk = block_keys(block_start)
        scores = block_scores(block_start, keys_blk)
        new_max = jnp.maximum(running_max, jnp.max(scores, axis=-1))
        running_sum = running_sum * jnp.exp(running_max - new_max) + jnp.sum(
            jnp.exp(scores - new_max[..., None]), axis=-1
        )
        return (new_max, running_sum)

    running_max, running_sum = lax.fori_loop(
        0,
        block_total,
        stats_step,
        (jnp.full(stat_shape, masked_score, jnp.float32), jnp.zeros(stat_shape, jnp.float32)),
    )
    log_total = running_max + jnp.log(running_sum)

    def output_step(block_index, accum_in):
        block_start = block_index * key_block
        keys_blk, values_blk = block_keys(block_start)
        prob_blk = jnp.exp(block_scores(block_start, keys_blk) - log_total[..., None]).astype(
            jnp.bfloat16
        )
        return accum_in + jnp.einsum(
            "rhgqk,rkhd->rqhgd", prob_blk, values_blk, preferred_element_type=jnp.float32
        )

    attended = lax.fori_loop(
        0,
        block_total,
        output_step,
        jnp.zeros((rows_here, seg_tok, heads_kv, grouping, head_dim), jnp.float32),
    )
    attended_b = attended.reshape(tokens_here, heads_query * head_dim).astype(jnp.bfloat16)
    middle = residual + jnp.dot(attended_b, out_full, preferred_element_type=jnp.float32)
    ffn_here = w_gate.shape[1] // 2

    def ffn_columns(weight):
        first, second = weight[:, :ffn_here], weight[:, ffn_here:]
        keep = jnp.where(y_at == 0, first, second)
        send = jnp.where(y_at == 0, second, first)
        block = in_order(keep, y_swap(send), y_at, 0).reshape(-1, ffn_here)
        return jnp.concatenate(ring_gather(block), axis=0)

    def ffn_rows(weight):
        first, second = weight[:ffn_here], weight[ffn_here:]
        keep = jnp.where(y_at == 0, first, second)
        send = jnp.where(y_at == 0, second, first)
        block = in_order(keep, y_swap(send), y_at, 1).reshape(ffn_here, -1)
        return jnp.concatenate(ring_gather(block), axis=1)

    gate_loc, up_loc, down_loc = ffn_columns(w_gate), ffn_columns(w_up), ffn_rows(w_down)
    plane_width = feature_count // planes
    ffn_in = rms_apply(middle, ffn_gain_full).astype(jnp.bfloat16)
    grad_top_b = cotangent.reshape(tokens_here, feature_count)
    ffn_all = gather_tokens(turn_columns(ffn_in, z_at, plane_width))
    cot_all = gather_tokens(turn_columns(grad_top_b, z_at, plane_width))
    z_back = (planes - z_at) % planes
    gate_val = jnp.dot(ffn_all, gate_loc, preferred_element_type=jnp.float32)
    up_val = jnp.dot(ffn_all, up_loc, preferred_element_type=jnp.float32)
    hidden_b = (jax.nn.silu(gate_val) * up_val).astype(jnp.bfloat16)
    down_terms = jnp.dot(hidden_b, down_loc, preferred_element_type=jnp.float32)
    down_mine = turn_columns(scatter_tokens(down_terms), z_back, plane_width)
    output = middle + down_mine
    output_b = output.astype(jnp.bfloat16).reshape(rows_here, seg_tok, feature_count)
    grad_hidden = times_transposed(cot_all, down_loc)
    grad_down_w = transposed_times(hidden_b, cot_all)
    sigma_gate = jax.nn.sigmoid(gate_val)
    grad_gate_b = (
        grad_hidden * up_val * sigma_gate * (1.0 + gate_val * (1.0 - sigma_gate))
    ).astype(jnp.bfloat16)
    grad_up_b = (grad_hidden * gate_val * sigma_gate).astype(jnp.bfloat16)
    ffn_in_terms = times_transposed(grad_gate_b, gate_loc) + times_transposed(grad_up_b, up_loc)
    grad_gate_w = transposed_times(ffn_all, grad_gate_b)
    grad_up_w = transposed_times(ffn_all, grad_up_b)

    def columns_home(grad):
        low = grad.astype(jnp.bfloat16).reshape(planes, plane_width, ffn_here)
        mine = ring_scatter([low[t] for t in range(planes)]).reshape(2, -1, ffn_here)
        keep, send = pick(mine, y_at, 0)
        got = y_swap(send.astype(jnp.bfloat16)).astype(jnp.float32)
        return in_order(keep, got, y_at, 1).reshape(-1, 2 * ffn_here)

    def rows_home(grad):
        low = grad.astype(jnp.bfloat16)
        mine = ring_scatter(
            [low[:, t * plane_width : (t + 1) * plane_width] for t in range(planes)]
        )
        first, second = mine[:, : plane_width // 2], mine[:, plane_width // 2 :]
        keep = jnp.where(y_at == 0, first, second)
        send = jnp.where(y_at == 0, second, first)
        got = y_swap(send.astype(jnp.bfloat16)).astype(jnp.float32)
        return in_order(keep, got, y_at, 0).reshape(2 * ffn_here, -1)

    ffn_sums = (columns_home(grad_gate_w), columns_home(grad_up_w), rows_home(grad_down_w))
    grad_ffn_in = turn_columns(scatter_tokens(ffn_in_terms), z_back, plane_width)
    grad_mid_ffn, gain_ffn_rows = rms_back(middle, ffn_gain_full, grad_ffn_in)
    grad_middle = grad_top_b.astype(jnp.float32) + grad_mid_ffn
    grad_gain_ffn = jnp.sum(gain_ffn_rows, axis=0)
    grad_branch = grad_middle.astype(jnp.bfloat16)
    grad_out_w = transposed_times(attended_b, grad_branch)
    grad_attended = times_transposed(grad_branch, out_full).astype(jnp.bfloat16)
    grad_att = grad_attended.reshape(rows_here, seg_tok, heads_kv, grouping, head_dim)

    def delta_step(block_index, accum_in):
        block_start = block_index * key_block
        keys_blk, values_blk = block_keys(block_start)
        prob_blk = jnp.exp(block_scores(block_start, keys_blk) - log_total[..., None])
        grad_probs = jnp.einsum(
            "rqhgd,rkhd->rhgqk", grad_att, values_blk, preferred_element_type=jnp.float32
        )
        return accum_in + jnp.sum(prob_blk * grad_probs, axis=-1)

    delta_row = lax.fori_loop(0, block_total, delta_step, jnp.zeros(stat_shape, jnp.float32))
    kv_shape = (rows_here, row_len, heads_kv, head_dim)

    def grad_step(block_index, state_in):
        grad_query_acc, grad_keys_acc, grad_values_acc = state_in
        block_start = block_index * key_block
        keys_blk, values_blk = block_keys(block_start)
        prob_blk = jnp.exp(block_scores(block_start, keys_blk) - log_total[..., None])
        grad_probs = jnp.einsum(
            "rqhgd,rkhd->rhgqk", grad_att, values_blk, preferred_element_type=jnp.float32
        )
        grad_scores = (prob_blk * (grad_probs - delta_row[..., None])).astype(jnp.bfloat16)
        grad_query_acc = (
            grad_query_acc
            + jnp.einsum(
                "rhgqk,rkhd->rqhgd", grad_scores, keys_blk, preferred_element_type=jnp.float32
            )
            * score_scale
        )
        key_part = (
            jnp.einsum(
                "rhgqk,rqhgd->rkhd", grad_scores, query_b, preferred_element_type=jnp.float32
            )
            * score_scale
        )
        value_part = jnp.einsum(
            "rhgqk,rqhgd->rkhd",
            prob_blk.astype(jnp.bfloat16),
            grad_att,
            preferred_element_type=jnp.float32,
        )
        grad_keys_acc = lax.dynamic_update_slice_in_dim(grad_keys_acc, key_part, block_start, 1)
        grad_values_acc = lax.dynamic_update_slice_in_dim(
            grad_values_acc, value_part, block_start, 1
        )
        return (grad_query_acc, grad_keys_acc, grad_values_acc)

    grad_query_rot, grad_keys_full, grad_values_full = lax.fori_loop(
        0,
        block_total,
        grad_step,
        (
            jnp.zeros((rows_here, seg_tok, heads_kv, grouping, head_dim), jnp.float32),
            jnp.zeros(kv_shape, jnp.float32),
            jnp.zeros(kv_shape, jnp.float32),
        ),
    )
    grad_kv = jnp.concatenate(
        [
            grad_keys_full.reshape(rows_here, row_len, -1),
            grad_values_full.reshape(rows_here, row_len, -1),
        ],
        axis=2,
    ).astype(jnp.bfloat16)
    grad_kv = jnp.moveaxis(grad_kv.reshape(rows_here, planes, 2, seg_tok, kv_width), 0, 2)
    keep, send = pick(grad_kv, y_at, 1)
    grad_kv = turn(add_low(keep, y_swap(send)), z_at)
    grad_kv_mine = ring_scatter([grad_kv[t] for t in range(planes)])
    grad_keys_mine = grad_kv_mine[..., : kv_width // 2]
    grad_values_mine = grad_kv_mine[..., kv_width // 2 :]
    grad_value_b = grad_values_mine.reshape(tokens_here, heads_kv * head_dim).astype(jnp.bfloat16)
    grad_key_norm = rotate_back(
        grad_keys_mine.reshape(tokens_here, heads_kv, head_dim), cosine, sine
    )
    grad_key_pre, gain_k_rows = rms_back(key_heads, gain_k, grad_key_norm)
    grad_key_b = grad_key_pre.reshape(tokens_here, heads_kv * head_dim).astype(jnp.bfloat16)
    grad_query_norm = rotate_back(
        grad_query_rot.reshape(tokens_here, heads_query, head_dim), cosine, sine
    )
    grad_query_pre, gain_q_rows = rms_back(query_heads, gain_q, grad_query_norm)
    grad_query_b = grad_query_pre.reshape(tokens_here, heads_query * head_dim).astype(jnp.bfloat16)
    grad_qkv_b = jnp.concatenate([grad_query_b, grad_key_b, grad_value_b], axis=1)
    grad_qkv_w = transposed_times(normed, grad_qkv_b)
    grad_normed = times_transposed(grad_qkv_b, qkv_full)
    grad_resid_attn, gain_attn_rows = rms_back(
        residual, attn_gain_full, grad_normed
    )
    grad_inputs = (grad_middle + grad_resid_attn).reshape(rows_here, seg_tok, feature_count)
    grad_gain_attn = jnp.sum(gain_attn_rows, axis=0)
    grad_qkv_mine = jnp.concatenate(
        [
            scatter_weights(grad_qkv_w[:, :qkv_cut], True),
            scatter_weights(grad_qkv_w[:, qkv_cut:], False),
        ],
        axis=1,
    )
    grad_out_mine = jnp.concatenate(
        [
            scatter_weights(grad_out_w[:, :out_cut], True),
            scatter_weights(grad_out_w[:, out_cut:], False),
        ],
        axis=1,
    )
    small = jnp.concatenate(
        [
            grad_gain_attn,
            grad_gain_ffn,
            jnp.sum(gain_q_rows, axis=(0, 1)),
            jnp.sum(gain_k_rows, axis=(0, 1)),
        ]
    )
    small = sum_all(small.reshape(-1, 128)).reshape(-1)
    return (
        output_b,
        grad_inputs,
        grad_qkv_mine[:, :width_q],
        grad_qkv_mine[:, width_q : width_q + width_k],
        grad_qkv_mine[:, width_q + width_k :],
        grad_out_mine,
        ffn_sums[0],
        ffn_sums[1],
        ffn_sums[2],
        lax.dynamic_slice_in_dim(small, place * gain_size, gain_size),
        small[2 * feature_count : 2 * feature_count + head_dim],
        small[2 * feature_count + head_dim :],
        lax.dynamic_slice_in_dim(small, feature_count + place * gain_size, gain_size),
    )


def solution(mesh):
    return jax.shard_map(
        local,
        mesh=mesh,
        in_specs=(
            P("rows", "seq", None),
            P("rows", "seq", None),
            P("rows", "seq"),
            P("rows", "seq"),
            P(("rows", "seq"), None),
            P(("rows", "seq"), None),
            P(("rows", "seq"), None),
            P(("rows", "seq"), None),
            P("seq", "rows"),
            P("seq", "rows"),
            P("rows", "seq"),
            P(("rows", "seq")),
            P(),
            P(),
            P(("rows", "seq")),
        ),
        out_specs=(
            P("rows", "seq", None),
            P("rows", "seq", None),
            P(("rows", "seq"), None),
            P(("rows", "seq"), None),
            P(("rows", "seq"), None),
            P(("rows", "seq"), None),
            P("seq", "rows"),
            P("seq", "rows"),
            P("rows", "seq"),
            P(("rows", "seq")),
            P(),
            P(),
            P(("rows", "seq")),
        ),
        check_vma=False,
    )
```

```python
import functools

import jax
import jax.numpy as jnp
from jax import lax
from jax.experimental import pallas as pl
from jax.experimental.pallas import tpu as pltpu
from jax.sharding import Mesh
from jax.sharding import PartitionSpec as P

norm_eps = 1e-06
masked_score = -1e30


def head_sums(values, head_dim):
    width = values.shape[1]
    row = lax.broadcasted_iota(jnp.int32, (width, width), 0) // head_dim
    column = lax.broadcasted_iota(jnp.int32, (width, width), 1) // head_dim
    ones = jnp.where(row == column, 1.0, 0.0).astype(jnp.bfloat16)
    total = None
    for _ in range(3):
        part = values.astype(jnp.bfloat16)
        values = values - part.astype(jnp.float32)
        term = jnp.dot(part, ones, preferred_element_type=jnp.float32)
        total = term if total is None else total + term
    return total


def half_turn(values, head_dim):
    half = head_dim // 2
    width = values.shape[1]
    lane = lax.broadcasted_iota(jnp.int32, values.shape, 1) % head_dim
    ahead = pltpu.roll(values, width - half, 1)
    behind = pltpu.roll(values, half, 1)
    return jnp.where(lane < half, ahead, behind)


def signed(sine, head_dim):
    lane = lax.broadcasted_iota(jnp.int32, sine.shape, 1) % head_dim
    return jnp.where(lane < head_dim // 2, -sine, sine)


def head_norm_rotate(values, gain, cosine, sine, head_dim):
    scale = lax.rsqrt(head_sums(values * values, head_dim) / head_dim + norm_eps)
    normed = values * scale * gain
    return normed * cosine + half_turn(normed, head_dim) * signed(sine, head_dim)


def head_norm_rotate_back(grad, values, gain, cosine, sine, head_dim):
    grad = grad * cosine - half_turn(grad * sine, head_dim) * signed(
        jnp.ones_like(sine), head_dim
    )
    scale = lax.rsqrt(head_sums(values * values, head_dim) / head_dim + norm_eps)
    weighted = grad * gain
    inner = head_sums(weighted * values, head_dim)
    back = scale * weighted - values * (scale * scale * scale) * inner / head_dim
    return back, grad * values * scale


def wide(table, count):
    return jnp.concatenate([table] * count, axis=1)


def fill_mask(pieces, row, base_ref, segq_ref, segk_ref, mask_ref):
    size = segq_ref.shape[1]
    seg_query = segq_ref[pl.ds(row, 1), :]
    query_at = base_ref[0] + lax.broadcasted_iota(jnp.int32, (size, size), 1)
    for piece in range(pieces):
        count = segk_ref.shape[0] // segq_ref.shape[0]
        line = segk_ref[pl.ds(row * count + base_ref[1 + piece] // size, 1), :]
        seg_key = jnp.broadcast_to(line, (size, size)).astype(jnp.float32).T
        key_at = base_ref[1 + piece] + lax.broadcasted_iota(jnp.int32, (size, size), 0)
        allowed = (key_at <= query_at) & (
            seg_key == jnp.broadcast_to(seg_query, (size, size)).astype(jnp.float32)
        )
        mask_ref[piece * size : (piece + 1) * size, :] = jnp.where(allowed, 0.0, masked_score)


def attend_kernel(pieces, heads_kv, grouping, base_ref, q_ref, segq_ref, segk_ref, *refs):
    kv_refs = refs[:pieces]
    out_ref, log_ref, q_heads, k_heads, v_heads, mask_ref = refs[pieces:]
    row, group = pl.program_id(0), pl.program_id(1)
    size, head_dim = segq_ref.shape[1], k_heads.shape[2]

    @pl.when(group == 0)
    def _():
        for head in range(heads_kv):
            for j in range(grouping):
                at = (head * grouping + j) * head_dim
                q_heads[head, j * size : (j + 1) * size, :] = q_ref[:, at : at + head_dim]
            for piece in range(pieces):
                rows = slice(piece * size, (piece + 1) * size)
                at = head * head_dim
                k_heads[head, rows, :] = kv_refs[piece][:, at : at + head_dim]
                at += heads_kv * head_dim
                v_heads[head, rows, :] = kv_refs[piece][:, at : at + head_dim]
        fill_mask(pieces, row, base_ref, segq_ref, segk_ref, mask_ref)

    together = grouping if pieces <= 8 else 1
    turned = []
    for first in range(0, grouping, together):
        rows = slice(first * size, (first + together) * size)
        scores = lax.dot_general(
            k_heads[group], q_heads[group, rows, :], NT, preferred_element_type=jnp.float32
        ) + wide(mask_ref[...], together)
        top = jnp.max(scores, axis=0, keepdims=True)
        probs = jnp.exp(scores - top)
        total = jnp.sum(probs, axis=0, keepdims=True)
        probs_b = (probs * (1.0 / total)).astype(jnp.bfloat16)
        mixed = lax.dot_general(
            v_heads[group], probs_b, (((0,), (0,)), ((), ())), preferred_element_type=jnp.float32
        )
        turned += [mixed[:, j * size : (j + 1) * size].T for j in range(together)]
        log_ref[:, rows] = top + jnp.log(total)
    out_ref[...] = jnp.concatenate(turned, axis=1).astype(jnp.bfloat16)


def attend_call(heads_kv, grouping, bases, query_b, seg_here, seg_all, kv_pieces):
    pieces = len(kv_pieces)
    rows, size = seg_here.shape
    head_dim = kv_pieces[0].shape[1] // (2 * heads_kv)
    block = grouping * head_dim
    width = heads_kv * block
    keys = pieces * size
    row_block = lambda w: pl.BlockSpec((size, w), lambda r, g: (r, 0))
    whole = lambda a: pl.BlockSpec(a.shape, lambda r, g: (0,) * a.ndim)
    low, full = jnp.bfloat16, jnp.float32
    return pl.pallas_call(
        functools.partial(attend_kernel, pieces, heads_kv, grouping),
        grid=(rows, heads_kv),
        out_shape=[
            jax.ShapeDtypeStruct((rows * size, width), low),
            jax.ShapeDtypeStruct((rows, heads_kv, 1, grouping * size), full),
        ],
        in_specs=[
            pl.BlockSpec(memory_space=pltpu.SMEM),
            row_block(width),
            whole(seg_here),
            whole(seg_all),
        ]
        + [row_block(2 * heads_kv * head_dim)] * pieces,
        out_specs=[
            pl.BlockSpec((size, block), lambda r, g: (r, g)),
            pl.BlockSpec((None, None, 1, grouping * size), lambda r, g: (r, g, 0, 0)),
        ],
        scratch_shapes=[
            pltpu.VMEM((heads_kv, grouping * size, head_dim), low),
            pltpu.VMEM((heads_kv, keys, head_dim), low),
            pltpu.VMEM((heads_kv, keys, head_dim), low),
            pltpu.VMEM((keys, size), full),
        ],
        compiler_params=pltpu.CompilerParams(vmem_limit_bytes=60 * 1024 * 1024),
        cost_estimate=pl.CostEstimate(
            flops=4 * rows * size * keys * width * 4,
            bytes_accessed=4 * rows * size * width + 4 * rows * keys * heads_kv * head_dim,
            transcendentals=rows * heads_kv * grouping * size * keys,
        ),
    )(bases, query_b, seg_here, seg_all, *kv_pieces)


def attend_back_kernel(
    pieces,
    heads_kv,
    grouping,
    base_ref,
    q_ref,
    do_ref,
    segq_ref,
    segk_ref,
    log_ref,
    pre_ref,
    gain_ref,
    cos_ref,
    sin_ref,
    *refs,
):
    kv_refs = refs[:pieces]
    dq_ref, gain_rows_ref = refs[pieces : pieces + 2]
    dkv_refs = refs[pieces + 2 : 2 * pieces + 2]
    q_heads, do_heads, k_heads, v_heads, dk_heads, dv_heads, mask_ref = refs[2 * pieces + 2 :]
    row, group = pl.program_id(0), pl.program_id(1)
    size, head_dim = segq_ref.shape[1], k_heads.shape[2]

    @pl.when(group == 0)
    def _():
        for head in range(heads_kv):
            for j in range(grouping):
                at = (head * grouping + j) * head_dim
                q_heads[head, j * size : (j + 1) * size, :] = q_ref[:, at : at + head_dim]
                do_heads[head, j * size : (j + 1) * size, :] = do_ref[:, at : at + head_dim]
            for piece in range(pieces):
                rows = slice(piece * size, (piece + 1) * size)
                at = head * head_dim
                k_heads[head, rows, :] = kv_refs[piece][:, at : at + head_dim]
                at += heads_kv * head_dim
                v_heads[head, rows, :] = kv_refs[piece][:, at : at + head_dim]
        fill_mask(pieces, row, base_ref, segq_ref, segk_ref, mask_ref)

    together = grouping if pieces <= 8 else 1
    turned = []
    for first in range(0, grouping, together):
        rows = slice(first * size, (first + together) * size)
        queries, grads = q_heads[group, rows, :], do_heads[group, rows, :]
        scores = lax.dot_general(
            k_heads[group], queries, NT, preferred_element_type=jnp.float32
        ) + wide(mask_ref[...], together)
        probs = jnp.exp(scores - log_ref[:, rows])
        grad_probs = lax.dot_general(
            v_heads[group], grads, NT, preferred_element_type=jnp.float32
        )
        grad_values = jnp.dot(
            probs.astype(jnp.bfloat16), grads, preferred_element_type=jnp.float32
        )
        delta = jnp.sum(probs * grad_probs, axis=0, keepdims=True)
        grad_scores = (probs * (grad_probs - delta)).astype(jnp.bfloat16)
        grad_keys = jnp.dot(grad_scores, queries, preferred_element_type=jnp.float32)
        if first:
            grad_values = grad_values + dv_heads[group].astype(jnp.float32)
            grad_keys = grad_keys + dk_heads[group].astype(jnp.float32)
        dv_heads[group] = grad_values.astype(dv_heads.dtype)
        dk_heads[group] = grad_keys.astype(dk_heads.dtype)
        mixed = lax.dot_general(
            k_heads[group], grad_scores, (((0,), (0,)), ((), ())), preferred_element_type=jnp.float32
        ) * (head_dim**-0.5)
        turned += [mixed[:, j * size : (j + 1) * size].T for j in range(together)]
    grad_query = jnp.concatenate(turned, axis=1)
    copies = grad_query.shape[1] // cos_ref.shape[1]
    back, gain_rows = head_norm_rotate_back(
        grad_query,
        pre_ref[...],
        gain_ref[...],
        wide(cos_ref[...], copies),
        wide(sin_ref[...], copies),
        head_dim,
    )
    dq_ref[...] = back.astype(jnp.bfloat16)
    gain_rows_ref[...] = jnp.sum(gain_rows, axis=0, keepdims=True)

    @pl.when(group == heads_kv - 1)
    def _():
        for piece in range(pieces):
            rows = slice(piece * size, (piece + 1) * size)
            dkv_refs[piece][...] = jnp.concatenate(
                [dk_heads[head, rows, :] for head in range(heads_kv)]
                + [dv_heads[head, rows, :] for head in range(heads_kv)],
                axis=1,
            )


def attend_back_call(
    heads_kv, grouping, bases, query_b, grad_att, seg_here, seg_all, logs, query_pre, gain, cosine, sine, kv_pieces
):
    pieces = len(kv_pieces)
    rows, size = seg_here.shape
    head_dim = kv_pieces[0].shape[1] // (2 * heads_kv)
    block = grouping * head_dim
    width = heads_kv * block
    keys = pieces * size
    kv_width = 2 * heads_kv * head_dim
    row_block = lambda w: pl.BlockSpec((size, w), lambda r, g: (r, 0))
    column_block = pl.BlockSpec((size, block), lambda r, g: (r, g))
    whole = lambda a: pl.BlockSpec(a.shape, lambda r, g: (0,) * a.ndim)
    low, full = jnp.bfloat16, jnp.float32
    heads = lambda n, t: pltpu.VMEM((heads_kv, n, head_dim), t)
    return pl.pallas_call(
        functools.partial(attend_back_kernel, pieces, heads_kv, grouping),
        grid=(rows, heads_kv),
        out_shape=[
            jax.ShapeDtypeStruct((rows * size, width), low),
            jax.ShapeDtypeStruct((rows, heads_kv, 1, block), full),
        ]
        + [jax.ShapeDtypeStruct((rows * size, kv_width), low)] * pieces,
        in_specs=[
            pl.BlockSpec(memory_space=pltpu.SMEM),
            row_block(width),
            row_block(width),
            whole(seg_here),
            whole(seg_all),
            pl.BlockSpec((None, None, 1, grouping * size), lambda r, g: (r, g, 0, 0)),
            column_block,
            whole(gain),
            row_block(cosine.shape[1]),
            row_block(sine.shape[1]),
        ]
        + [row_block(kv_width)] * pieces,
        out_specs=[
            column_block,
            pl.BlockSpec((None, None, 1, block), lambda r, g: (r, g, 0, 0)),
        ]
        + [row_block(kv_width)] * pieces,
        scratch_shapes=[
            heads(grouping * size, low),
            heads(grouping * size, low),
            heads(keys, low),
            heads(keys, low),
            heads(keys, low),
            heads(keys, low),
            pltpu.VMEM((keys, size), full),
        ],
        compiler_params=pltpu.CompilerParams(vmem_limit_bytes=60 * 1024 * 1024),
        cost_estimate=pl.CostEstimate(
            flops=10 * rows * size * keys * width * 4,
            bytes_accessed=8 * rows * size * width + 8 * rows * keys * heads_kv * head_dim,
            transcendentals=rows * heads_kv * grouping * size * keys,
        ),
    )(bases, query_b, grad_att, seg_here, seg_all, logs, query_pre, gain, cosine, sine, *kv_pieces)


def place_copies(spots, pieces, place_ref, w_ref, sems):
    x_at, core_at, z_at, y_at = [place_ref[i] for i in range(4)]
    copies = []
    for index, (dx, dy, dc, column) in enumerate(spots):
        piece = pieces[index]
        planes, size, width = piece.shape
        for t in range(planes):
            row = (x_at + dx - 2 * x_at * dx) * 2 + (core_at + dc - 2 * core_at * dc)
            row = (row * planes + lax.rem(z_at + t, planes)) * 2 + (y_at + dy - 2 * y_at * dy)
            start = pl.multiple_of(row * size, size)
            copies.append(
                pltpu.make_async_copy(
                    piece.at[t],
                    w_ref.at[pl.ds(start, size), column : column + width],
                    sems.at[index, t],
                )
            )
    return copies


def project_kernel(width_q, head_dim, spots, place_ref, x_ref, gain_ref, gq_ref, gk_ref, cos_ref, sin_ref, *refs):
    pieces, outs, (w_ref, sems) = refs[: len(spots)], refs[len(spots) : -2], refs[-2:]
    copies_in = place_copies(spots, pieces, place_ref, w_ref, sems)
    for copy in copies_in:
        copy.start()
    normed_ref, pre_ref, kpre_ref, q_ref, kv_ref = outs
    values = x_ref[...].astype(jnp.float32)
    scale = lax.rsqrt(jnp.mean(values * values, axis=1, keepdims=True) + norm_eps)
    normed_ref[...] = (values * scale * gain_ref[...]).astype(jnp.bfloat16)
    block = 256
    cosine, sine = cos_ref[...], sin_ref[...]
    for copy in copies_in:
        copy.wait()
    total = w_ref.shape[1]
    for first in range(0, width_q, block):
        pre = jnp.dot(
            normed_ref[...], w_ref[:, first : first + block], preferred_element_type=jnp.float32
        )
        pre_ref[:, first : first + block] = pre
        copies = block // cosine.shape[1]
        rotated = head_norm_rotate(
            pre, gq_ref[...], wide(cosine, copies), wide(sine, copies), head_dim
        )
        q_ref[:, first : first + block] = (rotated * (head_dim**-0.5)).astype(jnp.bfloat16)
    pre = jnp.dot(normed_ref[...], w_ref[:, width_q:], preferred_element_type=jnp.float32)
    kpre_ref[...] = pre
    copies = pre.shape[1] // cosine.shape[1]
    rotated = head_norm_rotate(pre, gk_ref[...], wide(cosine, copies), wide(sine, copies), head_dim)
    lane = lax.broadcasted_iota(jnp.int32, pre.shape, 1)
    kv_ref[...] = jnp.where(lane < pre.shape[1] // 2, rotated, pre).astype(jnp.bfloat16)


def project_call(width_q, head_dim, total, place, x, gain, gain_q, gain_k, cosine, sine, spots, pieces):
    tokens, features = x.shape
    kv = total - width_q
    low, full = jnp.bfloat16, jnp.float32
    vm = pl.BlockSpec(memory_space=pltpu.VMEM)
    return pl.pallas_call(
        functools.partial(project_kernel, width_q, head_dim, spots),
        out_shape=[
            jax.ShapeDtypeStruct((tokens, features), low),
            jax.ShapeDtypeStruct((tokens, width_q), full),
            jax.ShapeDtypeStruct((tokens, kv), full),
            jax.ShapeDtypeStruct((tokens, width_q), low),
            jax.ShapeDtypeStruct((tokens, kv), low),
        ],
        in_specs=[pl.BlockSpec(memory_space=pltpu.SMEM)]
        + [vm] * 6
        + [pl.BlockSpec(memory_space=pl.ANY)] * len(pieces),
        out_specs=[vm] * 5,
        scratch_shapes=[
            pltpu.VMEM((features, total), low),
            pltpu.SemaphoreType.DMA((len(pieces), pieces[0].shape[0])),
        ],
        compiler_params=pltpu.CompilerParams(vmem_limit_bytes=60 * 1024 * 1024),
        cost_estimate=pl.CostEstimate(
            flops=2 * tokens * features * total,
            bytes_accessed=2 * features * total + 10 * tokens * features,
            transcendentals=tokens,
        ),
    )(place, x, gain, gain_q, gain_k, cosine, sine, *pieces)


def keys_back_kernel(head_dim, grad_ref, kpre_ref, gk_ref, cos_ref, sin_ref, out_ref, gain_rows_ref):
    grad = grad_ref[...]
    copies = grad.shape[1] // cos_ref.shape[1]
    back, gain_rows = head_norm_rotate_back(
        grad,
        kpre_ref[...],
        gk_ref[...],
        wide(cos_ref[...], copies),
        wide(sin_ref[...], copies),
        head_dim,
    )
    lane = lax.broadcasted_iota(jnp.int32, grad.shape, 1)
    out_ref[...] = jnp.where(lane < grad.shape[1] // 2, back, grad).astype(jnp.bfloat16)
    gain_rows_ref[...] = jnp.sum(gain_rows, axis=0, keepdims=True)


def keys_back_call(head_dim, grad, kpre, gain_k, cosine, sine):
    vm = pl.BlockSpec(memory_space=pltpu.VMEM)
    return pl.pallas_call(
        functools.partial(keys_back_kernel, head_dim),
        out_shape=[
            jax.ShapeDtypeStruct(grad.shape, jnp.bfloat16),
            jax.ShapeDtypeStruct((1, grad.shape[1]), jnp.float32),
        ],
        in_specs=[vm] * 5,
        out_specs=[vm] * 2,
        compiler_params=pltpu.CompilerParams(vmem_limit_bytes=60 * 1024 * 1024),
    )(grad, kpre, gain_k, cosine, sine)


def input_kernel(spots, place_ref, g_ref, x_ref, gain_ref, mid_ref, *refs):
    pieces = refs[: len(spots)]
    out_ref, gain_rows_ref, w_ref, sems = refs[len(spots) :]
    copies = place_copies(spots, pieces, place_ref, w_ref, sems)
    for copy in copies:
        copy.start()
    values = x_ref[...].astype(jnp.float32)
    scale = lax.rsqrt(jnp.mean(values * values, axis=1, keepdims=True) + norm_eps)
    for copy in copies:
        copy.wait()
    grad = lax.dot_general(
        g_ref[...], w_ref[...], (((1,), (1,)), ((), ())), preferred_element_type=jnp.float32
    )
    weighted = grad * gain_ref[...]
    inner = jnp.sum(weighted * values, axis=1, keepdims=True)
    back = scale * weighted - values * (scale * scale * scale) * inner / values.shape[1]
    out_ref[...] = mid_ref[...] + back
    gain_rows_ref[...] = jnp.sum(grad * values * scale, axis=0, keepdims=True)


def input_call(place, grad_qkv, x, gain, grad_middle, spots, pieces):
    tokens, features = x.shape
    total = grad_qkv.shape[1]
    vm = pl.BlockSpec(memory_space=pltpu.VMEM)
    return pl.pallas_call(
        functools.partial(input_kernel, spots),
        out_shape=[
            jax.ShapeDtypeStruct((tokens, features), jnp.float32),
            jax.ShapeDtypeStruct((1, features), jnp.float32),
        ],
        in_specs=[pl.BlockSpec(memory_space=pltpu.SMEM)]
        + [vm] * 4
        + [pl.BlockSpec(memory_space=pl.ANY)] * len(pieces),
        out_specs=[vm] * 2,
        scratch_shapes=[
            pltpu.VMEM((features, total), jnp.bfloat16),
            pltpu.SemaphoreType.DMA((len(pieces), pieces[0].shape[0])),
        ],
        compiler_params=pltpu.CompilerParams(vmem_limit_bytes=60 * 1024 * 1024),
        cost_estimate=pl.CostEstimate(
            flops=2 * tokens * features * total,
            bytes_accessed=2 * features * total + 10 * tokens * features,
            transcendentals=tokens,
        ),
    )(place, grad_qkv, x, gain, grad_middle, *pieces)

ANY = pl.BlockSpec(memory_space=pl.ANY)
VMEM = pl.BlockSpec(memory_space=pltpu.VMEM)
SMEM = pl.BlockSpec(memory_space=pltpu.SMEM)
NT = (((1,), (1,)), ((), ()))


def params():
    return pltpu.CompilerParams(vmem_limit_bytes=60 * 1024 * 1024)


def cuts(total, step):
    edges = list(range(0, total - step // 2, step)) + [total]
    return list(zip(edges[:-1], edges[1:]))


def weight_copies(planes, gathered, which, target, sems):
    size = gathered.shape[2]
    return [
        pltpu.make_async_copy(
            gathered.at[core * planes + z, which],
            target.at[pl.ds((2 * z + core) * size, size)],
            sems.at[core * planes + z],
        )
        for core in range(2)
        for z in range(planes)
    ]


def ffn_kernel(planes, blocks, chained, place_ref, *refs):
    refs = list(refs)
    take = lambda n: [refs.pop(0) for _ in range(n)]
    x_refs, c_refs = take(blocks), take(blocks)
    before = take(blocks) if chained else None
    (gathered,) = take(1)
    outs = take(4 * blocks)
    weights, sems = refs
    copies = [
        weight_copies(planes, gathered, which, weights.at[which], sems.at[which])
        for which in range(3)
    ]
    for group in copies:
        for copy in group:
            copy.start()
    waiting = list(copies)

    def arrive():
        if waiting:
            for copy in waiting.pop(0):
                copy.wait()

    features, units = weights.shape[1:]
    for block in range(blocks):
        hidden_ref, dgate_ref, dup_ref, dx_ref = outs[4 * block : 4 * block + 4]
        for first, last in cuts(units, 512):
            arrive()
            gate = jnp.dot(
                x_refs[block][...], weights[0, :, first:last], preferred_element_type=jnp.float32
            )
            arrive()
            up = jnp.dot(
                x_refs[block][...], weights[1, :, first:last], preferred_element_type=jnp.float32
            )
            arrive()
            dh = jnp.dot(
                c_refs[block][...], weights[2, :, first:last], preferred_element_type=jnp.float32
            )
            sigma = 1.0 / (1.0 + jnp.exp(-gate))
            silu = gate * sigma
            hidden_ref[:, first:last] = (silu * up).astype(jnp.bfloat16)
            dup_ref[:, first:last] = (dh * silu).astype(jnp.bfloat16)
            dgate_ref[:, first:last] = (dh * up * (sigma + silu * (1.0 - sigma))).astype(
                jnp.bfloat16
            )
        for first, last in cuts(features, 512):
            dx = lax.dot_general(
                dgate_ref[...], weights[0, first:last], NT, preferred_element_type=jnp.float32
            ) + lax.dot_general(
                dup_ref[...], weights[1, first:last], NT, preferred_element_type=jnp.float32
            )
            if chained:
                dx = dx + before[block][:, first:last].astype(jnp.float32)
            dx_ref[:, first:last] = dx.astype(jnp.bfloat16)


def ffn_call(planes, place, xs, cs, gathered, before=None):
    blocks = len(xs)
    tokens, features = xs[0].shape
    units = gathered.shape[3]
    low = jnp.bfloat16
    one = [jax.ShapeDtypeStruct((tokens, units), low)] * 3 + [
        jax.ShapeDtypeStruct((tokens, features), low)
    ]
    chained = before is not None
    operands = [*xs, *cs, *(before or [])]
    return pl.pallas_call(
        functools.partial(ffn_kernel, planes, blocks, chained),
        out_shape=one * blocks,
        in_specs=[SMEM] + [VMEM] * len(operands) + [ANY],
        out_specs=[VMEM] * (4 * blocks),
        scratch_shapes=[
            pltpu.VMEM((3, features, units), low),
            pltpu.SemaphoreType.DMA((3, 2 * planes)),
        ],
        compiler_params=params(),
        cost_estimate=pl.CostEstimate(
            flops=10 * blocks * tokens * features * units,
            bytes_accessed=6 * features * units + 8 * blocks * tokens * features,
            transcendentals=blocks * tokens * units,
        ),
    )(place, *operands, gathered)


def weight_grad_kernel(blocks, place_ref, *refs):
    a_refs = [refs[:blocks], refs[blocks : 2 * blocks]]
    b_refs = [refs[(2 + i) * blocks : (3 + i) * blocks] for i in range(3)]
    own_ref, other_ref, turned = refs[5 * blocks :]
    size, units = own_ref.shape[1:]
    tokens = a_refs[0][0].shape[0]
    core_at = place_ref[1]
    for kind in range(2):
        for block in range(blocks):
            turned[kind, :, block * tokens : (block + 1) * tokens] = a_refs[kind][block][...].T
    for out_ref, half in ((other_ref, 1 - core_at), (own_ref, core_at)):
        rows = pl.ds(pl.multiple_of(half * size, size), size)
        for which in range(3):
            for first, last in cuts(units, 512):
                total = None
                for block in range(blocks):
                    part = jnp.dot(
                        turned[which // 2, rows, block * tokens : (block + 1) * tokens],
                        b_refs[which][block][:, first:last],
                        preferred_element_type=jnp.float32,
                    )
                    total = part if total is None else total + part
                out_ref[which, :, first:last] = total.astype(jnp.bfloat16)


def weight_grad_call(planes, place, xs, cs, dgates, dups, hiddens):
    blocks = len(xs)
    tokens, features = xs[0].shape
    units = dgates[0].shape[1]
    size = features // (2 * planes)
    out = jax.ShapeDtypeStruct((planes, 3, size, units), jnp.bfloat16)
    column = pl.BlockSpec((tokens, 2 * size), lambda t, place: (0, t))
    return pl.pallas_call(
        functools.partial(weight_grad_kernel, blocks),
        out_shape=[out, out],
        grid_spec=pltpu.PrefetchScalarGridSpec(
            num_scalar_prefetch=1,
            grid=(planes,),
            in_specs=[column] * (2 * blocks)
            + [pl.BlockSpec((tokens, units), lambda t, place: (0, 0))] * (3 * blocks),
            out_specs=[pl.BlockSpec((None, 3, size, units), lambda t, place: (t, 0, 0, 0))] * 2,
            scratch_shapes=[pltpu.VMEM((2, 2 * size, blocks * tokens), jnp.bfloat16)],
        ),
        compiler_params=params(),
        cost_estimate=pl.CostEstimate(
            flops=6 * blocks * tokens * features * units,
            bytes_accessed=6 * blocks * tokens * units + 6 * features * units,
            transcendentals=0,
        ),
    )(place, *xs, *cs, *dgates, *dups, *hiddens)


def down_kernel(planes, blocks, parts, place_ref, *refs):
    refs = list(refs)
    take = lambda n: [refs.pop(0) for _ in range(n)]
    h_refs = [take(blocks) for _ in range(parts)]
    gathered = take(parts)
    outs = take(blocks)
    weights = take(parts)
    (sems,) = refs
    copies = []
    for part in range(parts):
        copies += weight_copies(planes, gathered[part], 2, weights[part], sems.at[part])
    for copy in copies:
        copy.start()
    for copy in copies:
        copy.wait()
    for block in range(blocks):
        for first, last in cuts(weights[0].shape[0], 512):
            total = None
            for part in range(parts):
                term = lax.dot_general(
                    h_refs[part][block][...],
                    weights[part][first:last],
                    NT,
                    preferred_element_type=jnp.float32,
                )
                total = term if total is None else total + term
            outs[block][:, first:last] = total.astype(jnp.bfloat16)


def down_call(planes, place, hidden_parts, gathered_parts):
    parts, blocks = len(hidden_parts), len(hidden_parts[0])
    tokens = hidden_parts[0][0].shape[0]
    size = gathered_parts[0].shape[2]
    features = 2 * planes * size
    units = [h[0].shape[1] for h in hidden_parts]
    return pl.pallas_call(
        functools.partial(down_kernel, planes, blocks, parts),
        out_shape=[jax.ShapeDtypeStruct((tokens, features), jnp.bfloat16)] * blocks,
        in_specs=[SMEM] + [VMEM] * (parts * blocks) + [ANY] * parts,
        out_specs=[VMEM] * blocks,
        scratch_shapes=[pltpu.VMEM((features, n), jnp.bfloat16) for n in units]
        + [pltpu.SemaphoreType.DMA((parts, 2 * planes))],
        compiler_params=params(),
        cost_estimate=pl.CostEstimate(
            flops=2 * blocks * tokens * features * sum(units),
            bytes_accessed=2 * features * sum(units) + 8 * blocks * tokens * features,
            transcendentals=0,
        ),
    )(
        place,
        *[h for part in hidden_parts for h in part],
        *gathered_parts,
    )


def rms_apply(values, gain_vec):
    row_scale = lax.rsqrt(jnp.mean(values * values, axis=-1, keepdims=True) + norm_eps)
    return values * row_scale * gain_vec


def rms_back(values, gain_vec, grad_in):
    row_scale = lax.rsqrt(jnp.mean(values * values, axis=-1, keepdims=True) + norm_eps)
    weighted = grad_in * gain_vec
    inner_sum = jnp.sum(weighted * values, axis=-1, keepdims=True)
    grad_values = (
        row_scale * weighted
        - values * (row_scale * row_scale * row_scale) * inner_sum / values.shape[-1]
    )
    return (grad_values, grad_in * values * row_scale)


def rotary_tables(positions, head_dim):
    half_dim = head_dim // 2
    frequencies = 10000.0 ** (-2.0 * jnp.arange(half_dim).astype(jnp.float32) / head_dim)
    angles = positions.astype(jnp.float32)[..., None] * frequencies
    angles = jnp.concatenate([angles, angles], axis=-1)
    return (jnp.cos(angles), jnp.sin(angles))


def times_transposed(left, right):
    return lax.dot_general(
        left, right, (((1,), (1,)), ((), ())), preferred_element_type=jnp.float32
    )


def transposed_times(left, right):
    return lax.dot_general(
        left, right, (((0,), (0,)), ((), ())), preferred_element_type=jnp.float32
    )


def swap(values, axis_name, bit):
    count = lax.axis_size(axis_name)
    return lax.ppermute(values, axis_name, [(i, i ^ bit) for i in range(count)])


def ring(values, shift):
    count = lax.axis_size("z")
    return lax.ppermute(values, "z", [(i, (i + shift) % count) for i in range(count)])


def core_swap(values):
    return swap(values, "core", 1)


def x_swap(values):
    return swap(values, "x", 1)


def y_swap(values):
    return swap(values, "y", 1)


def sum_over(values, names):
    for axis_name in names:
        bit = 1
        while bit < lax.axis_size(axis_name):
            values = values + swap(values, axis_name, bit)
            bit *= 2
    return values


def places():
    return tuple(lax.axis_index(name) for name in ("x", "core", "z", "y"))


def in_order(first, other, bit, axis):
    return jnp.where(
        bit == 0, jnp.stack([first, other], axis=axis), jnp.stack([other, first], axis=axis)
    )


def corner(values):
    moved = lax.ppermute(values, ("core", "y"), [(1, 2), (2, 1)])
    return jnp.where(lax.axis_index("core") == lax.axis_index("y"), values, moved)


def chain(values, shift):
    count = lax.axis_size("z")
    moves = [(i, i + shift) for i in range(count) if 0 <= i + shift < count]
    return lax.ppermute(values, "z", moves)


def hold(values, *others):
    return lax.optimization_barrier((values, *others))[0]


def together(*values):
    return lax.optimization_barrier(values)


def ring_gather(values):
    pieces = [values]
    for _ in range(lax.axis_size("z") - 1):
        pieces.append(ring(pieces[-1], -1))
    return pieces


def direct_gather(values):
    return [values] + [ring(values, -t) for t in range(1, lax.axis_size("z"))]


def ring_scatter(pieces):
    count = len(pieces)
    moving = None
    for step in range(1, count):
        block = pieces[count - step]
        if moving is not None:
            block = (block.astype(jnp.float32) + moving.astype(jnp.float32)).astype(jnp.bfloat16)
        moving = ring(block, 1)
    return pieces[0].astype(jnp.float32) + moving.astype(jnp.float32)


def turn(values, start):
    count = values.shape[0]
    return lax.dynamic_slice_in_dim(jnp.concatenate([values, values], axis=0), start, count, 0)


def turn_columns(values, start, width):
    return lax.dynamic_slice_in_dim(
        jnp.concatenate([values, values], axis=1), start * width, values.shape[1], 1
    )


def pick(values, bit, axis):
    return (
        lax.dynamic_index_in_dim(values, bit, axis, keepdims=False),
        lax.dynamic_index_in_dim(values, 1 - bit, axis, keepdims=False),
    )


def add_low(left, right):
    return (left.astype(jnp.float32) + right.astype(jnp.float32)).astype(jnp.bfloat16)


def gather_tokens(values):
    half = values.shape[1] // 2
    from_x = x_swap(values)
    from_y = y_swap(values)
    from_xy = jnp.concatenate([y_swap(from_x[:, :half]), x_swap(from_y[:, half:])], axis=1)
    return [values, from_x, from_y, from_xy]


def scatter_tokens(blocks):
    own, to_x, to_y, to_xy = blocks
    half = own.shape[1] // 2
    via_x = x_swap(to_xy[:, :half])
    via_y = y_swap(to_xy[:, half:])
    to_y = jnp.concatenate([add_low(to_y[:, :half], via_x), to_y[:, half:]], axis=1)
    to_x = jnp.concatenate([to_x[:, :half], add_low(to_x[:, half:], via_y)], axis=1)
    return (
        own.astype(jnp.float32)
        + x_swap(to_x).astype(jnp.float32)
        + y_swap(to_y).astype(jnp.float32)
    )


def local(
    inputs,
    cotangent,
    positions,
    segment_ids,
    w_query,
    w_key,
    w_value,
    w_out,
    w_gate,
    w_up,
    w_down,
    gain_attn,
    gain_query,
    gain_key,
    gain_ffn,
):
    rows_here, seg_tok, feature_count = inputs.shape
    tokens_here = rows_here * seg_tok
    head_dim = gain_query.shape[0]
    heads_query = w_query.shape[1] // head_dim
    heads_kv = w_key.shape[1] // head_dim
    grouping = heads_query // heads_kv
    planes = lax.axis_size("z")
    rows_count, seq_count = 4, 2 * planes
    row_len = seg_tok * seq_count
    x_at, core_at, z_at, y_at = places()
    seq_place = 2 * z_at + y_at
    row_place = 2 * x_at + core_at
    device = row_place * seq_count + seq_place
    place = jnp.stack([x_at, core_at, z_at, y_at]).astype(jnp.int32)
    gain_size = gain_attn.shape[0]
    width_q, width_k = w_query.shape[1], w_key.shape[1]
    low = jnp.bfloat16

    shared = jnp.zeros((2 * feature_count + rows_count * rows_here * row_len,), jnp.float32)

    def put(shared, values, start):
        return lax.dynamic_update_slice_in_dim(shared, values.astype(jnp.float32), start, 0)

    shared = put(shared, gain_attn, device * gain_size)
    shared = put(shared, gain_ffn, feature_count + device * gain_size)
    for row in range(rows_here):
        start = ((row_place * rows_here + row) * seq_count + seq_place) * seg_tok
        shared = put(shared, segment_ids[row], 2 * feature_count + start)
    shared = shared.reshape(-1, 128)
    shared = shared + x_swap(shared)
    shared = shared + y_swap(shared)
    cotangent_here = cotangent.reshape(tokens_here, feature_count)
    cot_own = hold(cotangent_here, shared)
    cot_x, cot_y = x_swap(cot_own), y_swap(cot_own)
    shared = sum_over(shared, ("core", "z"))
    qkv_here = jnp.concatenate([w_query, w_key, w_value], axis=1)
    qkv_own, shared = together(jnp.stack(direct_gather(qkv_here)), shared)
    shared = shared.reshape(-1)
    attn_gain = shared[:feature_count].reshape(1, -1)
    ffn_gain = shared[feature_count : 2 * feature_count].reshape(1, -1)
    seg_all = shared[2 * feature_count :].reshape(rows_count, rows_here * seq_count, seg_tok)
    seg_all = lax.dynamic_index_in_dim(seg_all, row_place, 0, keepdims=False)
    seg_here = segment_ids.astype(jnp.float32)

    qkv_width = qkv_own.shape[2]
    cut = 1024
    out_own = turn(jnp.stack(direct_gather(w_out)), (planes - z_at) % planes)
    qkv_x, qkv_y, out_own, cot_x, cot_y = together(
        x_swap(qkv_own), y_swap(qkv_own), out_own, cot_x, cot_y
    )
    down_turned = w_down.T
    ffn_width = w_gate.shape[1]
    ffn_cut = (ffn_width // 256 + 1) * 128
    stacks = [
        jnp.stack([w[:, first:last] for w in (w_gate, w_up, down_turned)])
        for first, last in ((0, ffn_cut), (ffn_cut, ffn_width))
    ]
    qkv_a, qkv_b, out_x, first_stack = together(
        y_swap(qkv_x[..., :cut]),
        x_swap(qkv_y[..., cut:]),
        x_swap(out_own),
        corner(hold(stacks[0], qkv_x)),
    )
    out_block = in_order(out_own, out_x, x_at, 0)
    qkv_pieces = [qkv_own, qkv_x, qkv_y, qkv_a, qkv_b]
    qkv_pieces += [core_swap(piece) for piece in qkv_pieces]
    spots = [(0, 0, 0, 0), (1, 0, 0, 0), (0, 1, 0, 0), (1, 1, 0, 0), (1, 1, 0, cut)]
    spots = tuple(spots + [(dx, dy, 1, column) for dx, dy, _, column in spots])
    gathered_first = lax.all_gather(first_stack, ("core", "z"), axis=0)

    inputs_here = inputs.reshape(tokens_here, feature_count)
    cosine, sine = rotary_tables(positions.reshape(tokens_here), head_dim)
    cosine = jnp.concatenate([cosine, cosine], axis=1)
    sine = jnp.concatenate([sine, sine], axis=1)
    gain_q = jnp.tile(gain_query.astype(jnp.float32), grouping).reshape(1, -1)
    gain_k = jnp.tile(gain_key.astype(jnp.float32), 2 * heads_kv).reshape(1, -1)
    normed, query_pre, kv_pre, query_b, kv_here = project_call(
        width_q, head_dim, qkv_width, place, inputs_here, attn_gain, gain_q, gain_k, cosine, sine,
        spots, qkv_pieces,
    )

    half = feature_count // 2
    near = y_swap(kv_here)
    *kv_far, out_y, cot_a, cot_b, second_stack = together(
        *[chain(kv_here, t) for t in range(1, planes)],
        y_swap(hold(out_block, kv_here)),
        y_swap(hold(cot_x[:, :half], kv_here)),
        x_swap(hold(cot_y[:, half:], kv_here)),
        corner(hold(stacks[1], kv_here)),
    )
    parts = [gathered_first, lax.all_gather(second_stack, ("core", "z"), axis=0)]
    out_block = in_order(out_block, out_y, y_at, 2)
    kv_own = [kv_here] + list(kv_far)
    *kv_other, out_core = together(
        near, *[y_swap(piece) for piece in kv_far], core_swap(out_block)
    )
    out_full = in_order(out_block, out_core, core_at, 1).reshape(-1, feature_count)
    cot_blocks = [cotangent_here, cot_x, cot_y, jnp.concatenate([cot_a, cot_b], axis=1)]
    kv_pieces, bases = [], [seq_place * seg_tok]
    for t in range(planes):
        for dy, piece in enumerate((kv_own[t], kv_other[t])):
            kv_pieces.append(piece)
            bases.append(((z_at - t + planes) % planes * 2 + (y_at + dy) % 2) * seg_tok)
    bases = jnp.stack(bases).astype(jnp.int32)
    attended_b, logs = attend_call(
        heads_kv, grouping, bases, query_b, seg_here, seg_all, kv_pieces
    )
    residual = inputs_here.astype(jnp.float32)
    middle = residual + jnp.dot(attended_b, out_full, preferred_element_type=jnp.float32)
    ffn_in = rms_apply(middle, ffn_gain).astype(low)
    ffn_blocks = gather_tokens(ffn_in)

    before, where = None, place
    hidden_parts, home, sums = [], [], []
    for gathered in parts:
        result = ffn_call(
            planes, where, ffn_blocks, cot_blocks, gathered, before
        )
        hiddens, dgates, dups, before = [result[i::4] for i in range(4)]
        hidden_parts.append(hiddens)
        own, other = weight_grad_call(
            planes, place, ffn_blocks, cot_blocks, dgates, dups, hiddens
        )
        both = add_low(own, core_swap(other))
        where = hold(place, both) if not sums else place
        sums.append(lax.psum_scatter(both, "z", scatter_dimension=0))
    home = [corner(mine).astype(jnp.float32) for mine in sums]
    grad_ffn_in = scatter_tokens(before)
    down_blocks = down_call(planes, hold(place, own), hidden_parts, parts)
    down_blocks = hold(tuple(down_blocks), grad_ffn_in)
    down_mine = scatter_tokens(down_blocks)
    home = jnp.concatenate(home, axis=2)
    output_b = (middle + down_mine).astype(low).reshape(inputs.shape)
    grad_ffn_in = hold(grad_ffn_in, both)
    grad_mid_ffn, gain_ffn_rows = rms_back(middle, ffn_gain, grad_ffn_in)
    grad_middle = cotangent_here.astype(jnp.float32) + grad_mid_ffn
    grad_gain_ffn = jnp.sum(gain_ffn_rows, axis=0)
    grad_branch = grad_middle.astype(low)
    grad_attended = times_transposed(grad_branch, out_full).astype(low)

    def over_core(grad):
        keep, send = pick(grad.reshape(2, 2, planes, 2, -1, grad.shape[1]), core_at, 1)
        return add_low(keep, core_swap(send))

    def over_x(block):
        keep, send = pick(block, x_at, 0)
        return add_low(keep, x_swap(send))

    def over_y(block, axis):
        keep, send = pick(block, y_at, axis)
        return add_low(keep, y_swap(send))

    def over_z(block):
        block = turn(block, z_at)
        total = block[0].astype(jnp.float32)
        for t in range(1, planes):
            total = total + ring(block[t], t).astype(jnp.float32)
        return total

    out_core = over_core(transposed_times(attended_b, grad_branch).astype(low))
    result = attend_back_call(
        heads_kv, grouping, hold(bases, out_core, sums[0], *down_blocks), query_b, grad_attended,
        seg_here, seg_all, logs, query_pre, gain_q, cosine, sine, kv_pieces,
    )
    grad_query_b, gain_q_rows, dkv = result[0], result[1], result[2:]
    query_core = over_core(transposed_times(normed, grad_query_b).astype(low))
    *pairs, query_core, out_x = together(
        *[add_low(dkv[2 * t], y_swap(dkv[2 * t + 1])) for t in range(planes)],
        query_core,
        over_x(hold(out_core, down_mine)),
    )
    *far, query_x, out_y = together(
        *[chain(pairs[t], -t) for t in range(1, planes)], over_x(query_core), over_y(out_x, 1)
    )
    moving = pairs[0].astype(jnp.float32)
    for piece in far:
        moving = moving + piece.astype(jnp.float32)
    moving = hold(moving, sums[1])
    grad_kv_b, gain_k_rows = keys_back_call(head_dim, moving, kv_pre, gain_k, cosine, sine)
    kv_core, query_y, grad_out_mine = together(
        over_core(transposed_times(normed, grad_kv_b).astype(low)),
        over_y(query_x, 1),
        over_z(out_y),
    )
    grad_qkv_b = jnp.concatenate([grad_query_b, grad_kv_b], axis=1)
    grad_inputs, grad_gain_attn = input_call(
        hold(place, kv_core), grad_qkv_b, inputs_here, attn_gain, grad_middle, spots,
        qkv_pieces,
    )
    kv_y, grad_query_mine = together(over_y(kv_core, 2), over_z(query_y))
    grad_kv_mine = over_z(over_x(kv_y))
    gain_q_rows = jnp.sum(gain_q_rows.reshape(-1, head_dim), axis=0)
    gain_k_rows = jnp.sum(gain_k_rows.reshape(-1, head_dim)[:heads_kv], axis=0)
    small = jnp.concatenate([grad_gain_attn.reshape(-1), grad_gain_ffn, gain_q_rows, gain_k_rows])
    small = sum_over(small.reshape(-1, 128), ("x", "y", "core", "z")).reshape(-1)
    return (
        output_b,
        grad_inputs.reshape(inputs.shape),
        grad_query_mine,
        grad_kv_mine[:, :width_k],
        grad_kv_mine[:, width_k:],
        grad_out_mine,
        home[0],
        home[1],
        home[2].T,
        lax.dynamic_slice_in_dim(small, device * gain_size, gain_size),
        small[2 * feature_count : 2 * feature_count + head_dim],
        small[2 * feature_count + head_dim :],
        lax.dynamic_slice_in_dim(small, feature_count + device * gain_size, gain_size),
    )


def solution(mesh):
    rows, seq = mesh.devices.shape
    grid = Mesh(mesh.devices.reshape(2, rows // 2, seq // 2, 2), ("x", "core", "z", "y"))
    return jax.shard_map(
        local,
        mesh=grid,
        in_specs=(
            P(("x", "core"), ("z", "y"), None),
            P(("x", "core"), ("z", "y"), None),
            P(("x", "core"), ("z", "y")),
            P(("x", "core"), ("z", "y")),
            P(("x", "core", "z", "y"), None),
            P(("x", "core", "z", "y"), None),
            P(("x", "core", "z", "y"), None),
            P(("x", "core", "z", "y"), None),
            P(("z", "y"), ("x", "core")),
            P(("z", "y"), ("x", "core")),
            P(("x", "core"), ("z", "y")),
            P(("x", "core", "z", "y")),
            P(),
            P(),
            P(("x", "core", "z", "y")),
        ),
        out_specs=(
            P(("x", "core"), ("z", "y"), None),
            P(("x", "core"), ("z", "y"), None),
            P(("x", "core", "z", "y"), None),
            P(("x", "core", "z", "y"), None),
            P(("x", "core", "z", "y"), None),
            P(("x", "core", "z", "y"), None),
            P(("z", "y"), ("x", "core")),
            P(("z", "y"), ("x", "core")),
            P(("x", "core"), ("z", "y")),
            P(("x", "core", "z", "y")),
            P(),
            P(),
            P(("x", "core", "z", "y")),
        ),
        check_vma=False,
    )
```

```python
import functools

import jax
import jax.numpy as jnp
from jax import lax
from jax.experimental import pallas as pl
from jax.experimental.pallas import tpu as pltpu
from jax.sharding import Mesh
from jax.sharding import PartitionSpec as P

norm_eps = 1e-06
masked_score = -1e30


def head_sums(values, head_dim):
    width = values.shape[1]
    row = lax.broadcasted_iota(jnp.int32, (width, width), 0) // head_dim
    column = lax.broadcasted_iota(jnp.int32, (width, width), 1) // head_dim
    ones = jnp.where(row == column, 1.0, 0.0).astype(jnp.bfloat16)
    total = None
    for _ in range(3):
        part = values.astype(jnp.bfloat16)
        values = values - part.astype(jnp.float32)
        term = jnp.dot(part, ones, preferred_element_type=jnp.float32)
        total = term if total is None else total + term
    return total


def half_turn(values, head_dim):
    half = head_dim // 2
    width = values.shape[1]
    lane = lax.broadcasted_iota(jnp.int32, values.shape, 1) % head_dim
    ahead = pltpu.roll(values, width - half, 1)
    behind = pltpu.roll(values, half, 1)
    return jnp.where(lane < half, ahead, behind)


def signed(sine, head_dim):
    lane = lax.broadcasted_iota(jnp.int32, sine.shape, 1) % head_dim
    return jnp.where(lane < head_dim // 2, -sine, sine)


def head_norm_rotate(values, gain, cosine, sine, head_dim):
    scale = lax.rsqrt(head_sums(values * values, head_dim) / head_dim + norm_eps)
    normed = values * scale * gain
    return normed * cosine + half_turn(normed, head_dim) * signed(sine, head_dim)


def head_norm_rotate_back(grad, values, gain, cosine, sine, head_dim):
    grad = grad * cosine - half_turn(grad * sine, head_dim) * signed(
        jnp.ones_like(sine), head_dim
    )
    scale = lax.rsqrt(head_sums(values * values, head_dim) / head_dim + norm_eps)
    weighted = grad * gain
    inner = head_sums(weighted * values, head_dim)
    back = scale * weighted - values * (scale * scale * scale) * inner / head_dim
    return back, grad * values * scale


def wide(table, count):
    return jnp.concatenate([table] * count, axis=1)


def fill_mask(pieces, row, base_ref, segq_ref, segk_ref, mask_ref):
    size = segq_ref.shape[1]
    seg_query = segq_ref[pl.ds(row, 1), :]
    query_at = base_ref[0] + lax.broadcasted_iota(jnp.int32, (size, size), 1)
    for piece in range(pieces):
        count = segk_ref.shape[0] // segq_ref.shape[0]
        line = segk_ref[pl.ds(row * count + base_ref[1 + piece] // size, 1), :]
        seg_key = jnp.broadcast_to(line, (size, size)).astype(jnp.float32).T
        key_at = base_ref[1 + piece] + lax.broadcasted_iota(jnp.int32, (size, size), 0)
        allowed = (key_at <= query_at) & (
            seg_key == jnp.broadcast_to(seg_query, (size, size)).astype(jnp.float32)
        )
        mask_ref[piece * size : (piece + 1) * size, :] = jnp.where(allowed, 0.0, masked_score)


def attend_kernel(pieces, heads_kv, grouping, base_ref, q_ref, segq_ref, segk_ref, *refs):
    kv_refs = refs[:pieces]
    out_ref, log_ref, q_heads, k_heads, v_heads, mask_ref = refs[pieces:]
    row, group = pl.program_id(0), pl.program_id(1)
    size, head_dim = segq_ref.shape[1], k_heads.shape[2]

    @pl.when(group == 0)
    def _():
        for head in range(heads_kv):
            for j in range(grouping):
                at = (head * grouping + j) * head_dim
                q_heads[head, j * size : (j + 1) * size, :] = q_ref[:, at : at + head_dim]
            for piece in range(pieces):
                rows = slice(piece * size, (piece + 1) * size)
                at = head * head_dim
                k_heads[head, rows, :] = kv_refs[piece][:, at : at + head_dim]
                at += heads_kv * head_dim
                v_heads[head, rows, :] = kv_refs[piece][:, at : at + head_dim]
        fill_mask(pieces, row, base_ref, segq_ref, segk_ref, mask_ref)

    together = grouping if pieces <= 8 else 1
    turned = []
    for first in range(0, grouping, together):
        rows = slice(first * size, (first + together) * size)
        scores = lax.dot_general(
            k_heads[group], q_heads[group, rows, :], NT, preferred_element_type=jnp.float32
        ) + wide(mask_ref[...], together)
        top = jnp.max(scores, axis=0, keepdims=True)
        probs = jnp.exp(scores - top)
        total = jnp.sum(probs, axis=0, keepdims=True)
        probs_b = (probs * (1.0 / total)).astype(jnp.bfloat16)
        mixed = lax.dot_general(
            v_heads[group], probs_b, (((0,), (0,)), ((), ())), preferred_element_type=jnp.float32
        )
        turned += [mixed[:, j * size : (j + 1) * size].T for j in range(together)]
        log_ref[:, rows] = top + jnp.log(total)
    out_ref[...] = jnp.concatenate(turned, axis=1).astype(jnp.bfloat16)


def attend_call(heads_kv, grouping, bases, query_b, seg_here, seg_all, kv_pieces):
    pieces = len(kv_pieces)
    rows, size = seg_here.shape
    head_dim = kv_pieces[0].shape[1] // (2 * heads_kv)
    block = grouping * head_dim
    width = heads_kv * block
    keys = pieces * size
    row_block = lambda w: pl.BlockSpec((size, w), lambda r, g: (r, 0))
    whole = lambda a: pl.BlockSpec(a.shape, lambda r, g: (0,) * a.ndim)
    low, full = jnp.bfloat16, jnp.float32
    return pl.pallas_call(
        functools.partial(attend_kernel, pieces, heads_kv, grouping),
        grid=(rows, heads_kv),
        out_shape=[
            jax.ShapeDtypeStruct((rows * size, width), low),
            jax.ShapeDtypeStruct((rows, heads_kv, 1, grouping * size), full),
        ],
        in_specs=[
            pl.BlockSpec(memory_space=pltpu.SMEM),
            row_block(width),
            whole(seg_here),
            whole(seg_all),
        ]
        + [row_block(2 * heads_kv * head_dim)] * pieces,
        out_specs=[
            pl.BlockSpec((size, block), lambda r, g: (r, g)),
            pl.BlockSpec((None, None, 1, grouping * size), lambda r, g: (r, g, 0, 0)),
        ],
        scratch_shapes=[
            pltpu.VMEM((heads_kv, grouping * size, head_dim), low),
            pltpu.VMEM((heads_kv, keys, head_dim), low),
            pltpu.VMEM((heads_kv, keys, head_dim), low),
            pltpu.VMEM((keys, size), full),
        ],
        compiler_params=pltpu.CompilerParams(vmem_limit_bytes=60 * 1024 * 1024),
        cost_estimate=pl.CostEstimate(
            flops=4 * rows * size * keys * width * 4,
            bytes_accessed=4 * rows * size * width + 4 * rows * keys * heads_kv * head_dim,
            transcendentals=rows * heads_kv * grouping * size * keys,
        ),
    )(bases, query_b, seg_here, seg_all, *kv_pieces)


def attend_back_kernel(
    row,
    pieces,
    heads_kv,
    grouping,
    base_ref,
    q_ref,
    do_ref,
    segq_ref,
    segk_ref,
    log_ref,
    pre_ref,
    gain_ref,
    cos_ref,
    sin_ref,
    *refs,
):
    kv_refs = refs[:pieces]
    dq_ref, gain_rows_ref = refs[pieces : pieces + 2]
    dkv_refs = refs[pieces + 2 : 2 * pieces + 2]
    q_heads, do_heads, k_heads, v_heads, dk_heads, dv_heads, mask_ref = refs[2 * pieces + 2 :]
    group = pl.program_id(0)
    size, head_dim = segq_ref.shape[1], k_heads.shape[2]

    @pl.when(group == 0)
    def _():
        for head in range(heads_kv):
            for j in range(grouping):
                at = (head * grouping + j) * head_dim
                q_heads[head, j * size : (j + 1) * size, :] = q_ref[:, at : at + head_dim]
                do_heads[head, j * size : (j + 1) * size, :] = do_ref[:, at : at + head_dim]
            for piece in range(pieces):
                rows = slice(piece * size, (piece + 1) * size)
                at = head * head_dim
                k_heads[head, rows, :] = kv_refs[piece][:, at : at + head_dim]
                at += heads_kv * head_dim
                v_heads[head, rows, :] = kv_refs[piece][:, at : at + head_dim]
        fill_mask(pieces, row, base_ref, segq_ref, segk_ref, mask_ref)

    together = grouping if pieces <= 8 else 1
    turned = []
    for first in range(0, grouping, together):
        rows = slice(first * size, (first + together) * size)
        queries, grads = q_heads[group, rows, :], do_heads[group, rows, :]
        scores = lax.dot_general(
            k_heads[group], queries, NT, preferred_element_type=jnp.float32
        ) + wide(mask_ref[...], together)
        probs = jnp.exp(scores - log_ref[:, rows])
        grad_probs = lax.dot_general(
            v_heads[group], grads, NT, preferred_element_type=jnp.float32
        )
        grad_values = jnp.dot(
            probs.astype(jnp.bfloat16), grads, preferred_element_type=jnp.float32
        )
        delta = jnp.sum(probs * grad_probs, axis=0, keepdims=True)
        grad_scores = (probs * (grad_probs - delta)).astype(jnp.bfloat16)
        grad_keys = jnp.dot(grad_scores, queries, preferred_element_type=jnp.float32)
        if first:
            grad_values = grad_values + dv_heads[group].astype(jnp.float32)
            grad_keys = grad_keys + dk_heads[group].astype(jnp.float32)
        dv_heads[group] = grad_values.astype(dv_heads.dtype)
        dk_heads[group] = grad_keys.astype(dk_heads.dtype)
        mixed = lax.dot_general(
            k_heads[group], grad_scores, (((0,), (0,)), ((), ())), preferred_element_type=jnp.float32
        ) * (head_dim**-0.5)
        turned += [mixed[:, j * size : (j + 1) * size].T for j in range(together)]
    grad_query = jnp.concatenate(turned, axis=1)
    copies = grad_query.shape[1] // cos_ref.shape[1]
    back, gain_rows = head_norm_rotate_back(
        grad_query,
        pre_ref[...],
        gain_ref[...],
        wide(cos_ref[...], copies),
        wide(sin_ref[...], copies),
        head_dim,
    )
    dq_ref[...] = back.astype(jnp.bfloat16)
    gain_rows_ref[...] = jnp.sum(gain_rows, axis=0, keepdims=True)

    @pl.when(group == heads_kv - 1)
    def _():
        for piece in range(pieces):
            rows = slice(piece * size, (piece + 1) * size)
            dkv_refs[piece][...] = jnp.concatenate(
                [dk_heads[head, rows, :] for head in range(heads_kv)]
                + [dv_heads[head, rows, :] for head in range(heads_kv)],
                axis=1,
            )


def attend_back_call(
    row, heads_kv, grouping, bases, query_b, grad_att, seg_here, seg_all, logs, query_pre, gain, cosine, sine, kv_pieces
):
    pieces = len(kv_pieces)
    rows, size = seg_here.shape
    head_dim = kv_pieces[0].shape[1] // (2 * heads_kv)
    block = grouping * head_dim
    width = heads_kv * block
    keys = pieces * size
    kv_width = 2 * heads_kv * head_dim
    row_block = lambda w: pl.BlockSpec((size, w), lambda g: (row, 0))
    whole = lambda a: pl.BlockSpec(a.shape, lambda g: (0,) * a.ndim)
    low, full = jnp.bfloat16, jnp.float32
    heads = lambda n, t: pltpu.VMEM((heads_kv, n, head_dim), t)
    return pl.pallas_call(
        functools.partial(attend_back_kernel, row, pieces, heads_kv, grouping),
        grid=(heads_kv,),
        out_shape=[
            jax.ShapeDtypeStruct((size, width), low),
            jax.ShapeDtypeStruct((heads_kv, 1, block), full),
        ]
        + [jax.ShapeDtypeStruct((size, kv_width), low)] * pieces,
        in_specs=[
            pl.BlockSpec(memory_space=pltpu.SMEM),
            row_block(width),
            row_block(width),
            whole(seg_here),
            whole(seg_all),
            pl.BlockSpec((None, None, 1, grouping * size), lambda g: (row, g, 0, 0)),
            pl.BlockSpec((size, block), lambda g: (row, g)),
            whole(gain),
            row_block(cosine.shape[1]),
            row_block(sine.shape[1]),
        ]
        + [row_block(kv_width)] * pieces,
        out_specs=[
            pl.BlockSpec((size, block), lambda g: (0, g)),
            pl.BlockSpec((None, 1, block), lambda g: (g, 0, 0)),
        ]
        + [pl.BlockSpec((size, kv_width), lambda g: (0, 0))] * pieces,
        scratch_shapes=[
            heads(grouping * size, low),
            heads(grouping * size, low),
            heads(keys, low),
            heads(keys, low),
            heads(keys, low),
            heads(keys, low),
            pltpu.VMEM((keys, size), full),
        ],
        compiler_params=pltpu.CompilerParams(vmem_limit_bytes=60 * 1024 * 1024),
        cost_estimate=pl.CostEstimate(
            flops=10 * size * keys * width * 4,
            bytes_accessed=8 * size * width + 8 * keys * heads_kv * head_dim,
            transcendentals=heads_kv * grouping * size * keys,
        ),
    )(bases, query_b, grad_att, seg_here, seg_all, logs, query_pre, gain, cosine, sine, *kv_pieces)


def place_copies(spots, pieces, place_ref, w_ref, sems):
    x_at, core_at, z_at, y_at = [place_ref[i] for i in range(4)]
    copies = []
    for index, (dx, dy, dc, column) in enumerate(spots):
        piece = pieces[index]
        planes, size, width = piece.shape
        for t in range(planes):
            row = (x_at + dx - 2 * x_at * dx) * 2 + (core_at + dc - 2 * core_at * dc)
            row = (row * planes + lax.rem(z_at + t, planes)) * 2 + (y_at + dy - 2 * y_at * dy)
            start = pl.multiple_of(row * size, size)
            copies.append(
                pltpu.make_async_copy(
                    piece.at[t],
                    w_ref.at[pl.ds(start, size), column : column + width],
                    sems.at[index, t],
                )
            )
    return copies


def project_kernel(width_q, head_dim, spots, place_ref, x_ref, gain_ref, gq_ref, gk_ref, cos_ref, sin_ref, *refs):
    pieces, outs, (w_ref, sems) = refs[: len(spots)], refs[len(spots) : -2], refs[-2:]
    copies_in = place_copies(spots, pieces, place_ref, w_ref, sems)
    for copy in copies_in:
        copy.start()
    normed_ref, pre_ref, kpre_ref, q_ref, kv_ref = outs
    values = x_ref[...].astype(jnp.float32)
    scale = lax.rsqrt(jnp.mean(values * values, axis=1, keepdims=True) + norm_eps)
    normed_ref[...] = (values * scale * gain_ref[...]).astype(jnp.bfloat16)
    block = 256
    cosine, sine = cos_ref[...], sin_ref[...]
    for copy in copies_in:
        copy.wait()
    total = w_ref.shape[1]
    for first in range(0, width_q, block):
        pre = jnp.dot(
            normed_ref[...], w_ref[:, first : first + block], preferred_element_type=jnp.float32
        )
        pre_ref[:, first : first + block] = pre
        copies = block // cosine.shape[1]
        rotated = head_norm_rotate(
            pre, gq_ref[...], wide(cosine, copies), wide(sine, copies), head_dim
        )
        q_ref[:, first : first + block] = (rotated * (head_dim**-0.5)).astype(jnp.bfloat16)
    pre = jnp.dot(normed_ref[...], w_ref[:, width_q:], preferred_element_type=jnp.float32)
    kpre_ref[...] = pre
    copies = pre.shape[1] // cosine.shape[1]
    rotated = head_norm_rotate(pre, gk_ref[...], wide(cosine, copies), wide(sine, copies), head_dim)
    lane = lax.broadcasted_iota(jnp.int32, pre.shape, 1)
    kv_ref[...] = jnp.where(lane < pre.shape[1] // 2, rotated, pre).astype(jnp.bfloat16)


def project_call(width_q, head_dim, total, place, x, gain, gain_q, gain_k, cosine, sine, spots, pieces):
    tokens, features = x.shape
    kv = total - width_q
    low, full = jnp.bfloat16, jnp.float32
    vm = pl.BlockSpec(memory_space=pltpu.VMEM)
    return pl.pallas_call(
        functools.partial(project_kernel, width_q, head_dim, spots),
        out_shape=[
            jax.ShapeDtypeStruct((tokens, features), low),
            jax.ShapeDtypeStruct((tokens, width_q), full),
            jax.ShapeDtypeStruct((tokens, kv), full),
            jax.ShapeDtypeStruct((tokens, width_q), low),
            jax.ShapeDtypeStruct((tokens, kv), low),
        ],
        in_specs=[pl.BlockSpec(memory_space=pltpu.SMEM)]
        + [vm] * 6
        + [pl.BlockSpec(memory_space=pl.ANY)] * len(pieces),
        out_specs=[vm] * 5,
        scratch_shapes=[
            pltpu.VMEM((features, total), low),
            pltpu.SemaphoreType.DMA((len(pieces), pieces[0].shape[0])),
        ],
        compiler_params=pltpu.CompilerParams(vmem_limit_bytes=60 * 1024 * 1024),
        cost_estimate=pl.CostEstimate(
            flops=2 * tokens * features * total,
            bytes_accessed=2 * features * total + 10 * tokens * features,
            transcendentals=tokens,
        ),
    )(place, x, gain, gain_q, gain_k, cosine, sine, *pieces)


def keys_back_kernel(head_dim, grad_ref, kpre_ref, gk_ref, cos_ref, sin_ref, out_ref, gain_rows_ref):
    grad = grad_ref[...]
    copies = grad.shape[1] // cos_ref.shape[1]
    back, gain_rows = head_norm_rotate_back(
        grad,
        kpre_ref[...],
        gk_ref[...],
        wide(cos_ref[...], copies),
        wide(sin_ref[...], copies),
        head_dim,
    )
    lane = lax.broadcasted_iota(jnp.int32, grad.shape, 1)
    out_ref[...] = jnp.where(lane < grad.shape[1] // 2, back, grad).astype(jnp.bfloat16)
    gain_rows_ref[...] = jnp.sum(gain_rows, axis=0, keepdims=True)


def keys_back_call(head_dim, grad, kpre, gain_k, cosine, sine):
    vm = pl.BlockSpec(memory_space=pltpu.VMEM)
    return pl.pallas_call(
        functools.partial(keys_back_kernel, head_dim),
        out_shape=[
            jax.ShapeDtypeStruct(grad.shape, jnp.bfloat16),
            jax.ShapeDtypeStruct((1, grad.shape[1]), jnp.float32),
        ],
        in_specs=[vm] * 5,
        out_specs=[vm] * 2,
        compiler_params=pltpu.CompilerParams(vmem_limit_bytes=60 * 1024 * 1024),
    )(grad, kpre, gain_k, cosine, sine)


def input_kernel(spots, place_ref, g_ref, x_ref, gain_ref, mid_ref, *refs):
    pieces = refs[: len(spots)]
    out_ref, gain_rows_ref, w_ref, sems = refs[len(spots) :]
    copies = place_copies(spots, pieces, place_ref, w_ref, sems)
    for copy in copies:
        copy.start()
    values = x_ref[...].astype(jnp.float32)
    scale = lax.rsqrt(jnp.mean(values * values, axis=1, keepdims=True) + norm_eps)
    for copy in copies:
        copy.wait()
    grad = lax.dot_general(
        g_ref[...], w_ref[...], (((1,), (1,)), ((), ())), preferred_element_type=jnp.float32
    )
    weighted = grad * gain_ref[...]
    inner = jnp.sum(weighted * values, axis=1, keepdims=True)
    back = scale * weighted - values * (scale * scale * scale) * inner / values.shape[1]
    out_ref[...] = mid_ref[...] + back
    gain_rows_ref[...] = jnp.sum(grad * values * scale, axis=0, keepdims=True)


def input_call(place, grad_qkv, x, gain, grad_middle, spots, pieces):
    tokens, features = x.shape
    total = grad_qkv.shape[1]
    vm = pl.BlockSpec(memory_space=pltpu.VMEM)
    return pl.pallas_call(
        functools.partial(input_kernel, spots),
        out_shape=[
            jax.ShapeDtypeStruct((tokens, features), jnp.float32),
            jax.ShapeDtypeStruct((1, features), jnp.float32),
        ],
        in_specs=[pl.BlockSpec(memory_space=pltpu.SMEM)]
        + [vm] * 4
        + [pl.BlockSpec(memory_space=pl.ANY)] * len(pieces),
        out_specs=[vm] * 2,
        scratch_shapes=[
            pltpu.VMEM((features, total), jnp.bfloat16),
            pltpu.SemaphoreType.DMA((len(pieces), pieces[0].shape[0])),
        ],
        compiler_params=pltpu.CompilerParams(vmem_limit_bytes=60 * 1024 * 1024),
        cost_estimate=pl.CostEstimate(
            flops=2 * tokens * features * total,
            bytes_accessed=2 * features * total + 10 * tokens * features,
            transcendentals=tokens,
        ),
    )(place, grad_qkv, x, gain, grad_middle, *pieces)

ANY = pl.BlockSpec(memory_space=pl.ANY)
VMEM = pl.BlockSpec(memory_space=pltpu.VMEM)
SMEM = pl.BlockSpec(memory_space=pltpu.SMEM)
NT = (((1,), (1,)), ((), ()))


def params():
    return pltpu.CompilerParams(vmem_limit_bytes=60 * 1024 * 1024)


def cuts(total, step):
    edges = list(range(0, total - step // 2, step)) + [total]
    return list(zip(edges[:-1], edges[1:]))


def weight_copies(planes, gathered, which, target, sems):
    size = gathered.shape[2]
    return [
        pltpu.make_async_copy(
            gathered.at[core * planes + z, which],
            target.at[pl.ds((2 * z + core) * size, size)],
            sems.at[core * planes + z],
        )
        for core in range(2)
        for z in range(planes)
    ]


def ffn_kernel(planes, blocks, chained, place_ref, *refs):
    refs = list(refs)
    take = lambda n: [refs.pop(0) for _ in range(n)]
    x_refs, c_refs = take(blocks), take(blocks)
    before = take(blocks) if chained else None
    (gathered,) = take(1)
    outs = take(4 * blocks)
    weights, sems = refs
    copies = [
        weight_copies(planes, gathered, which, weights.at[which], sems.at[which])
        for which in range(3)
    ]
    for group in copies:
        for copy in group:
            copy.start()
    waiting = list(copies)

    def arrive():
        if waiting:
            for copy in waiting.pop(0):
                copy.wait()

    features, units = weights.shape[1:]
    for block in range(blocks):
        hidden_ref, dgate_ref, dup_ref, dx_ref = outs[4 * block : 4 * block + 4]
        for first, last in cuts(units, 512):
            arrive()
            gate = jnp.dot(
                x_refs[block][...], weights[0, :, first:last], preferred_element_type=jnp.float32
            )
            arrive()
            up = jnp.dot(
                x_refs[block][...], weights[1, :, first:last], preferred_element_type=jnp.float32
            )
            arrive()
            dh = jnp.dot(
                c_refs[block][...], weights[2, :, first:last], preferred_element_type=jnp.float32
            )
            sigma = 1.0 / (1.0 + jnp.exp(-gate))
            silu = gate * sigma
            hidden_ref[:, first:last] = (silu * up).astype(jnp.bfloat16)
            dup_ref[:, first:last] = (dh * silu).astype(jnp.bfloat16)
            dgate_ref[:, first:last] = (dh * up * (sigma + silu * (1.0 - sigma))).astype(
                jnp.bfloat16
            )
        for first, last in cuts(features, 512):
            dx = lax.dot_general(
                dgate_ref[...], weights[0, first:last], NT, preferred_element_type=jnp.float32
            ) + lax.dot_general(
                dup_ref[...], weights[1, first:last], NT, preferred_element_type=jnp.float32
            )
            if chained:
                dx = dx + before[block][:, first:last].astype(jnp.float32)
            dx_ref[:, first:last] = dx.astype(jnp.bfloat16)


def ffn_call(planes, place, xs, cs, gathered, before=None):
    blocks = len(xs)
    tokens, features = xs[0].shape
    units = gathered.shape[3]
    low = jnp.bfloat16
    one = [jax.ShapeDtypeStruct((tokens, units), low)] * 3 + [
        jax.ShapeDtypeStruct((tokens, features), low)
    ]
    chained = before is not None
    operands = [*xs, *cs, *(before or [])]
    return pl.pallas_call(
        functools.partial(ffn_kernel, planes, blocks, chained),
        out_shape=one * blocks,
        in_specs=[SMEM] + [VMEM] * len(operands) + [ANY],
        out_specs=[VMEM] * (4 * blocks),
        scratch_shapes=[
            pltpu.VMEM((3, features, units), low),
            pltpu.SemaphoreType.DMA((3, 2 * planes)),
        ],
        compiler_params=params(),
        cost_estimate=pl.CostEstimate(
            flops=10 * blocks * tokens * features * units,
            bytes_accessed=6 * features * units + 8 * blocks * tokens * features,
            transcendentals=blocks * tokens * units,
        ),
    )(place, *operands, gathered)


def weight_grad_kernel(blocks, place_ref, *refs):
    a_refs = [refs[:blocks], refs[blocks : 2 * blocks]]
    b_refs = [refs[(2 + i) * blocks : (3 + i) * blocks] for i in range(3)]
    own_ref, other_ref, turned = refs[5 * blocks :]
    size, units = own_ref.shape[1:]
    tokens = a_refs[0][0].shape[0]
    core_at = place_ref[1]
    for kind in range(2):
        for block in range(blocks):
            turned[kind, :, block * tokens : (block + 1) * tokens] = a_refs[kind][block][...].T
    for out_ref, half in ((other_ref, 1 - core_at), (own_ref, core_at)):
        rows = pl.ds(pl.multiple_of(half * size, size), size)
        for which in range(3):
            for first, last in cuts(units, 512):
                total = None
                for block in range(blocks):
                    part = jnp.dot(
                        turned[which // 2, rows, block * tokens : (block + 1) * tokens],
                        b_refs[which][block][:, first:last],
                        preferred_element_type=jnp.float32,
                    )
                    total = part if total is None else total + part
                out_ref[which, :, first:last] = total.astype(jnp.bfloat16)


def weight_grad_call(planes, place, xs, cs, dgates, dups, hiddens):
    blocks = len(xs)
    tokens, features = xs[0].shape
    units = dgates[0].shape[1]
    size = features // (2 * planes)
    out = jax.ShapeDtypeStruct((planes, 3, size, units), jnp.bfloat16)
    column = pl.BlockSpec((tokens, 2 * size), lambda t, place: (0, t))
    return pl.pallas_call(
        functools.partial(weight_grad_kernel, blocks),
        out_shape=[out, out],
        grid_spec=pltpu.PrefetchScalarGridSpec(
            num_scalar_prefetch=1,
            grid=(planes,),
            in_specs=[column] * (2 * blocks)
            + [pl.BlockSpec((tokens, units), lambda t, place: (0, 0))] * (3 * blocks),
            out_specs=[pl.BlockSpec((None, 3, size, units), lambda t, place: (t, 0, 0, 0))] * 2,
            scratch_shapes=[pltpu.VMEM((2, 2 * size, blocks * tokens), jnp.bfloat16)],
        ),
        compiler_params=params(),
        cost_estimate=pl.CostEstimate(
            flops=6 * blocks * tokens * features * units,
            bytes_accessed=6 * blocks * tokens * units + 6 * features * units,
            transcendentals=0,
        ),
    )(place, *xs, *cs, *dgates, *dups, *hiddens)


def down_kernel(planes, blocks, parts, place_ref, *refs):
    refs = list(refs)
    take = lambda n: [refs.pop(0) for _ in range(n)]
    h_refs = [take(blocks) for _ in range(parts)]
    gathered = take(parts)
    outs = take(blocks)
    weights = take(parts)
    (sems,) = refs
    copies = []
    for part in range(parts):
        copies += weight_copies(planes, gathered[part], 2, weights[part], sems.at[part])
    for copy in copies:
        copy.start()
    for copy in copies:
        copy.wait()
    for block in range(blocks):
        for first, last in cuts(weights[0].shape[0], 512):
            total = None
            for part in range(parts):
                term = lax.dot_general(
                    h_refs[part][block][...],
                    weights[part][first:last],
                    NT,
                    preferred_element_type=jnp.float32,
                )
                total = term if total is None else total + term
            outs[block][:, first:last] = total.astype(jnp.bfloat16)


def down_call(planes, place, hidden_parts, gathered_parts):
    parts, blocks = len(hidden_parts), len(hidden_parts[0])
    tokens = hidden_parts[0][0].shape[0]
    size = gathered_parts[0].shape[2]
    features = 2 * planes * size
    units = [h[0].shape[1] for h in hidden_parts]
    return pl.pallas_call(
        functools.partial(down_kernel, planes, blocks, parts),
        out_shape=[jax.ShapeDtypeStruct((tokens, features), jnp.bfloat16)] * blocks,
        in_specs=[SMEM] + [VMEM] * (parts * blocks) + [ANY] * parts,
        out_specs=[VMEM] * blocks,
        scratch_shapes=[pltpu.VMEM((features, n), jnp.bfloat16) for n in units]
        + [pltpu.SemaphoreType.DMA((parts, 2 * planes))],
        compiler_params=params(),
        cost_estimate=pl.CostEstimate(
            flops=2 * blocks * tokens * features * sum(units),
            bytes_accessed=2 * features * sum(units) + 8 * blocks * tokens * features,
            transcendentals=0,
        ),
    )(
        place,
        *[h for part in hidden_parts for h in part],
        *gathered_parts,
    )


def rms_apply(values, gain_vec):
    row_scale = lax.rsqrt(jnp.mean(values * values, axis=-1, keepdims=True) + norm_eps)
    return values * row_scale * gain_vec


def rms_back(values, gain_vec, grad_in):
    row_scale = lax.rsqrt(jnp.mean(values * values, axis=-1, keepdims=True) + norm_eps)
    weighted = grad_in * gain_vec
    inner_sum = jnp.sum(weighted * values, axis=-1, keepdims=True)
    grad_values = (
        row_scale * weighted
        - values * (row_scale * row_scale * row_scale) * inner_sum / values.shape[-1]
    )
    return (grad_values, grad_in * values * row_scale)


def rotary_tables(positions, head_dim):
    half_dim = head_dim // 2
    frequencies = 10000.0 ** (-2.0 * jnp.arange(half_dim).astype(jnp.float32) / head_dim)
    angles = positions.astype(jnp.float32)[..., None] * frequencies
    angles = jnp.concatenate([angles, angles], axis=-1)
    return (jnp.cos(angles), jnp.sin(angles))


def times_transposed(left, right):
    return lax.dot_general(
        left, right, (((1,), (1,)), ((), ())), preferred_element_type=jnp.float32
    )


def transposed_times(left, right):
    return lax.dot_general(
        left, right, (((0,), (0,)), ((), ())), preferred_element_type=jnp.float32
    )


def swap(values, axis_name, bit):
    count = lax.axis_size(axis_name)
    return lax.ppermute(values, axis_name, [(i, i ^ bit) for i in range(count)])


def ring(values, shift):
    count = lax.axis_size("z")
    return lax.ppermute(values, "z", [(i, (i + shift) % count) for i in range(count)])


def core_swap(values):
    return swap(values, "core", 1)


def x_swap(values):
    return swap(values, "x", 1)


def y_swap(values):
    return swap(values, "y", 1)


def sum_over(values, names):
    for axis_name in names:
        bit = 1
        while bit < lax.axis_size(axis_name):
            values = values + swap(values, axis_name, bit)
            bit *= 2
    return values


def places():
    return tuple(lax.axis_index(name) for name in ("x", "core", "z", "y"))


def in_order(first, other, bit, axis):
    return jnp.where(
        bit == 0, jnp.stack([first, other], axis=axis), jnp.stack([other, first], axis=axis)
    )


def corner(values):
    moved = lax.ppermute(values, ("core", "y"), [(1, 2), (2, 1)])
    return jnp.where(lax.axis_index("core") == lax.axis_index("y"), values, moved)


def chain(values, shift):
    count = lax.axis_size("z")
    moves = [(i, i + shift) for i in range(count) if 0 <= i + shift < count]
    return lax.ppermute(values, "z", moves)


def hold(values, *others):
    return lax.optimization_barrier((values, *others))[0]


def together(*values):
    return lax.optimization_barrier(values)


def ring_gather(values):
    pieces = [values]
    for _ in range(lax.axis_size("z") - 1):
        pieces.append(ring(pieces[-1], -1))
    return pieces


def direct_gather(values):
    return [values] + [ring(values, -t) for t in range(1, lax.axis_size("z"))]


def ring_scatter(pieces):
    count = len(pieces)
    moving = None
    for step in range(1, count):
        block = pieces[count - step]
        if moving is not None:
            block = (block.astype(jnp.float32) + moving.astype(jnp.float32)).astype(jnp.bfloat16)
        moving = ring(block, 1)
    return pieces[0].astype(jnp.float32) + moving.astype(jnp.float32)


def turn(values, start):
    count = values.shape[0]
    return lax.dynamic_slice_in_dim(jnp.concatenate([values, values], axis=0), start, count, 0)


def turn_columns(values, start, width):
    return lax.dynamic_slice_in_dim(
        jnp.concatenate([values, values], axis=1), start * width, values.shape[1], 1
    )


def pick(values, bit, axis):
    return (
        lax.dynamic_index_in_dim(values, bit, axis, keepdims=False),
        lax.dynamic_index_in_dim(values, 1 - bit, axis, keepdims=False),
    )


def add_low(left, right):
    return (left.astype(jnp.float32) + right.astype(jnp.float32)).astype(jnp.bfloat16)


def gather_tokens(values):
    half = values.shape[1] // 2
    from_x = x_swap(values)
    from_y = y_swap(values)
    from_xy = jnp.concatenate([y_swap(from_x[:, :half]), x_swap(from_y[:, half:])], axis=1)
    return [values, from_x, from_y, from_xy]


def scatter_corner(blocks):
    half = blocks[3].shape[1] // 2
    return x_swap(blocks[3][:, :half]), y_swap(blocks[3][:, half:])


def scatter_sides(blocks, via_x, via_y):
    _, to_x, to_y, _ = blocks
    half = to_x.shape[1] // 2
    to_y = jnp.concatenate([add_low(to_y[:, :half], via_x), to_y[:, half:]], axis=1)
    to_x = jnp.concatenate([to_x[:, :half], add_low(to_x[:, half:], via_y)], axis=1)
    return x_swap(to_x), y_swap(to_y)


def scatter_total(blocks, from_x, from_y):
    return (
        blocks[0].astype(jnp.float32) + from_x.astype(jnp.float32) + from_y.astype(jnp.float32)
    )


def local(
    inputs,
    cotangent,
    positions,
    segment_ids,
    w_query,
    w_key,
    w_value,
    w_out,
    w_gate,
    w_up,
    w_down,
    gain_attn,
    gain_query,
    gain_key,
    gain_ffn,
):
    rows_here, seg_tok, feature_count = inputs.shape
    tokens_here = rows_here * seg_tok
    head_dim = gain_query.shape[0]
    heads_query = w_query.shape[1] // head_dim
    heads_kv = w_key.shape[1] // head_dim
    grouping = heads_query // heads_kv
    planes = lax.axis_size("z")
    rows_count, seq_count = 4, 2 * planes
    row_len = seg_tok * seq_count
    x_at, core_at, z_at, y_at = places()
    seq_place = 2 * z_at + y_at
    row_place = 2 * x_at + core_at
    device = row_place * seq_count + seq_place
    place = jnp.stack([x_at, core_at, z_at, y_at]).astype(jnp.int32)
    gain_size = gain_attn.shape[0]
    width_q, width_k = w_query.shape[1], w_key.shape[1]
    low = jnp.bfloat16

    shared = jnp.zeros((2 * feature_count + rows_count * rows_here * row_len,), jnp.float32)

    def put(shared, values, start):
        return lax.dynamic_update_slice_in_dim(shared, values.astype(jnp.float32), start, 0)

    shared = put(shared, gain_attn, device * gain_size)
    shared = put(shared, gain_ffn, feature_count + device * gain_size)
    for row in range(rows_here):
        start = ((row_place * rows_here + row) * seq_count + seq_place) * seg_tok
        shared = put(shared, segment_ids[row], 2 * feature_count + start)
    cotangent_here = cotangent.reshape(tokens_here, feature_count)
    shared = sum_over(shared.reshape(-1, 128), ("core", "z"))
    qkv_here = jnp.concatenate([w_query, w_key, w_value], axis=1)
    qkv_own, shared = together(
        jnp.stack(direct_gather(qkv_here)), sum_over(shared, ("x", "y"))
    )
    shared = shared.reshape(-1)
    attn_gain = shared[:feature_count].reshape(1, -1)
    ffn_gain = shared[feature_count : 2 * feature_count].reshape(1, -1)
    seg_all = shared[2 * feature_count :].reshape(rows_count, rows_here * seq_count, seg_tok)
    seg_all = lax.dynamic_index_in_dim(seg_all, row_place, 0, keepdims=False)
    seg_here = segment_ids.astype(jnp.float32)

    qkv_width = qkv_own.shape[2]
    cut = 512
    out_own = turn(jnp.stack(direct_gather(w_out)), (planes - z_at) % planes)
    qkv_x, qkv_y, out_own = together(x_swap(qkv_own), y_swap(qkv_own), out_own)
    down_turned = w_down.T
    ffn_width = w_gate.shape[1]
    ffn_cut = (ffn_width // 256 + 1) * 128
    stacks = [
        jnp.stack([w[:, first:last] for w in (w_gate, w_up, down_turned)])
        for first, last in ((0, ffn_cut), (ffn_cut, ffn_width))
    ]
    qkv_a, qkv_b, first_stack = together(
        y_swap(qkv_x[..., :cut]),
        x_swap(qkv_y[..., cut:]),
        corner(hold(stacks[0], qkv_x)),
    )
    qkv_pieces = [qkv_own, qkv_x, qkv_y, qkv_a, qkv_b]
    qkv_pieces += [core_swap(piece) for piece in qkv_pieces]
    spots = [(0, 0, 0, 0), (1, 0, 0, 0), (0, 1, 0, 0), (1, 1, 0, 0), (1, 1, 0, cut)]
    spots = tuple(spots + [(dx, dy, 1, column) for dx, dy, _, column in spots])
    gathered_first = lax.all_gather(first_stack, ("core", "z"), axis=0)

    inputs_here = inputs.reshape(tokens_here, feature_count)
    cosine, sine = rotary_tables(positions.reshape(tokens_here), head_dim)
    cosine = jnp.concatenate([cosine, cosine], axis=1)
    sine = jnp.concatenate([sine, sine], axis=1)
    gain_q = jnp.tile(gain_query.astype(jnp.float32), grouping).reshape(1, -1)
    gain_k = jnp.tile(gain_key.astype(jnp.float32), 2 * heads_kv).reshape(1, -1)
    normed, query_pre, kv_pre, query_b, kv_here = project_call(
        width_q, head_dim, qkv_width, place, inputs_here, attn_gain, gain_q, gain_k, cosine, sine,
        spots, qkv_pieces,
    )

    cot_own = hold(cotangent_here, kv_here)
    *kv_far, near, out_y, cot_x, cot_y = together(
        *[chain(kv_here, t) for t in range(1, planes)],
        y_swap(kv_here),
        y_swap(hold(out_own, kv_here)),
        x_swap(cot_own),
        y_swap(cot_own),
    )
    out_block = in_order(out_own, out_y, y_at, 1)
    kv_own = [kv_here] + list(kv_far)
    *kv_other, out_x, second_stack = together(
        *[y_swap(piece) for piece in kv_far],
        x_swap(out_block),
        corner(hold(stacks[1], kv_far[-1])),
    )
    parts = [gathered_first, lax.all_gather(second_stack, ("core", "z"), axis=0)]
    cot_xy = x_swap(hold(cot_y, out_x))
    kv_other = [near] + list(kv_other)
    out_block = in_order(out_block, out_x, x_at, 0)
    cot_blocks = [cotangent_here, cot_x, cot_y, cot_xy]
    kv_pieces, bases = [], [seq_place * seg_tok]
    for t in range(planes):
        for dy, piece in enumerate((kv_own[t], kv_other[t])):
            kv_pieces.append(piece)
            bases.append(((z_at - t + planes) % planes * 2 + (y_at + dy) % 2) * seg_tok)
    bases = jnp.stack(bases).astype(jnp.int32)
    attended_b, logs = attend_call(
        heads_kv, grouping, bases, query_b, seg_here, seg_all, kv_pieces
    )
    attended_b, out_core = together(attended_b, core_swap(out_block))
    out_full = in_order(out_block, out_core, core_at, 1).reshape(-1, feature_count)
    residual = inputs_here.astype(jnp.float32)
    middle = residual + jnp.dot(attended_b, out_full, preferred_element_type=jnp.float32)
    ffn_in = rms_apply(middle, ffn_gain).astype(low)
    ffn_blocks = gather_tokens(hold(ffn_in, cot_xy))

    before, where = None, place
    hidden_parts, home, sums = [], [], []
    for gathered in parts:
        result = ffn_call(
            planes, where, ffn_blocks, cot_blocks, gathered, before
        )
        hiddens, dgates, dups, before = [result[i::4] for i in range(4)]
        hidden_parts.append(hiddens)
        own, other = weight_grad_call(
            planes, place, ffn_blocks, cot_blocks, dgates, dups, hiddens
        )
        both = add_low(own, core_swap(other))
        where = hold(place, both) if not sums else place
        sums.append(lax.psum_scatter(both, "z", scatter_dimension=0))
    via_x, via_y, last_own = together(*scatter_corner(before), own)
    from_x, from_y, both, *down_blocks = together(
        *scatter_sides(before, via_x, via_y),
        both,
        *down_call(planes, hold(place, last_own), hidden_parts, parts),
    )
    grad_ffn_in = scatter_total(before, from_x, from_y)
    grad_mid_ffn, gain_ffn_rows = rms_back(middle, ffn_gain, grad_ffn_in)
    grad_middle = cotangent_here.astype(jnp.float32) + grad_mid_ffn
    grad_gain_ffn = jnp.sum(gain_ffn_rows, axis=0)
    grad_branch = grad_middle.astype(low)
    grad_attended = times_transposed(grad_branch, out_full).astype(low)

    def over_core(grad):
        keep, send = pick(grad.reshape(2, 2, planes, 2, -1, grad.shape[1]), core_at, 1)
        return add_low(keep, core_swap(send))

    def over_x(block):
        keep, send = pick(block, x_at, 0)
        return add_low(keep, x_swap(send))

    def over_y(block, axis):
        keep, send = pick(block, y_at, axis)
        return add_low(keep, y_swap(send))

    def over_z(block):
        block = turn(block, z_at)
        total = block[0].astype(jnp.float32)
        for t in range(1, planes):
            total = total + ring(block[t], t).astype(jnp.float32)
        return total

    def back(row, bases):
        result = attend_back_call(
            row, heads_kv, grouping, bases, query_b, grad_attended, seg_here, seg_all, logs,
            query_pre, gain_q, cosine, sine, kv_pieces,
        )
        return result[0], result[1], result[2:]

    def over_pairs(dkv):
        return [add_low(dkv[2 * t], y_swap(dkv[2 * t + 1])) for t in range(planes)]

    def over_planes(pairs):
        return [pairs[0]] + [chain(pairs[t], -t) for t in range(1, planes)]

    grad_rows, gain_rows, pairs = [], [], []
    for row in range(rows_here):
        start = bases if row == 0 else hold(bases, grad_rows[-1])
        grad_row, gain_row, dkv = back(row, start)
        if row == 0:
            via_x, via_y, grad_row = together(*scatter_corner(down_blocks), grad_row)
        if row == 1:
            from_x, from_y, out_core, grad_row, *pairs[0] = together(
                *scatter_sides(down_blocks, via_x, via_y),
                over_core(
                    transposed_times(hold(attended_b, grad_rows[0]), grad_branch).astype(low)
                ),
                grad_row,
                *pairs[0],
            )
        grad_rows.append(grad_row)
        gain_rows.append(gain_row)
        pairs.append(over_pairs(dkv))
    down_mine = scatter_total(down_blocks, from_x, from_y)
    grad_query_b = jnp.concatenate(grad_rows, axis=0)
    gain_q_rows = jnp.stack(gain_rows)
    grad_query_w = transposed_times(normed, grad_query_b).astype(low)
    middle_q = width_q // 2
    *tied, query_a, query_b2, out_x, first_sum = together(
        *[piece for group in pairs[:-1] for piece in over_planes(group)],
        *pairs[-1],
        over_core(grad_query_w[:, :middle_q]),
        over_core(grad_query_w[:, middle_q:]),
        over_x(out_core),
        sums[0],
    )
    landed = [tied[i * planes : (i + 1) * planes] for i in range(rows_here)]
    *last, query_a, query_b2, out_y = together(
        *over_planes(landed[-1]), over_x(query_a), over_y(query_b2, 2), over_y(out_x, 1)
    )
    landed[-1] = last
    moving = []
    for pieces in landed:
        total = pieces[0].astype(jnp.float32)
        for piece in pieces[1:]:
            total = total + piece.astype(jnp.float32)
        moving.append(total)
    moving = jnp.concatenate(moving, axis=0)
    grad_kv_b, gain_k_rows = keys_back_call(head_dim, moving, kv_pre, gain_k, cosine, sine)
    kv_core, query_a, query_b2, grad_out_mine = together(
        over_core(transposed_times(normed, grad_kv_b).astype(low)),
        over_y(query_a, 1),
        over_x(query_b2),
        over_z(out_y),
    )
    grad_qkv_b = jnp.concatenate([grad_query_b, grad_kv_b], axis=1)
    grad_inputs, grad_gain_attn = input_call(
        hold(place, kv_core), grad_qkv_b, inputs_here, attn_gain, grad_middle, spots, qkv_pieces
    )
    kv_y, last_sum = together(over_y(kv_core, 2), sums[1])
    grad_kv_mine = over_z(over_x(kv_y))
    grad_query_mine = over_z(jnp.concatenate([query_a, query_b2], axis=2))
    home = [corner(mine).astype(jnp.float32) for mine in (first_sum, last_sum)]
    home = jnp.concatenate(home, axis=2)
    output_b = (middle + down_mine).astype(low).reshape(inputs.shape)
    gain_q_rows = jnp.sum(gain_q_rows.reshape(-1, head_dim), axis=0)
    gain_k_rows = jnp.sum(gain_k_rows.reshape(-1, head_dim)[:heads_kv], axis=0)
    small = jnp.concatenate([grad_gain_attn.reshape(-1), grad_gain_ffn, gain_q_rows, gain_k_rows])
    small = sum_over(small.reshape(-1, 128), ("x", "y", "core", "z")).reshape(-1)
    return (
        output_b,
        grad_inputs.reshape(inputs.shape),
        grad_query_mine,
        grad_kv_mine[:, :width_k],
        grad_kv_mine[:, width_k:],
        grad_out_mine,
        home[0],
        home[1],
        home[2].T,
        lax.dynamic_slice_in_dim(small, device * gain_size, gain_size),
        small[2 * feature_count : 2 * feature_count + head_dim],
        small[2 * feature_count + head_dim :],
        lax.dynamic_slice_in_dim(small, feature_count + device * gain_size, gain_size),
    )


def solution(mesh):
    rows, seq = mesh.devices.shape
    grid = Mesh(mesh.devices.reshape(2, rows // 2, seq // 2, 2), ("x", "core", "z", "y"))
    return jax.shard_map(
        local,
        mesh=grid,
        in_specs=(
            P(("x", "core"), ("z", "y"), None),
            P(("x", "core"), ("z", "y"), None),
            P(("x", "core"), ("z", "y")),
            P(("x", "core"), ("z", "y")),
            P(("x", "core", "z", "y"), None),
            P(("x", "core", "z", "y"), None),
            P(("x", "core", "z", "y"), None),
            P(("x", "core", "z", "y"), None),
            P(("z", "y"), ("x", "core")),
            P(("z", "y"), ("x", "core")),
            P(("x", "core"), ("z", "y")),
            P(("x", "core", "z", "y")),
            P(),
            P(),
            P(("x", "core", "z", "y")),
        ),
        out_specs=(
            P(("x", "core"), ("z", "y"), None),
            P(("x", "core"), ("z", "y"), None),
            P(("x", "core", "z", "y"), None),
            P(("x", "core", "z", "y"), None),
            P(("x", "core", "z", "y"), None),
            P(("x", "core", "z", "y"), None),
            P(("z", "y"), ("x", "core")),
            P(("z", "y"), ("x", "core")),
            P(("x", "core"), ("z", "y")),
            P(("x", "core", "z", "y")),
            P(),
            P(),
            P(("x", "core", "z", "y")),
        ),
        check_vma=False,
    )
```

```python
import functools

import jax
import jax.numpy as jnp
from jax import lax
from jax.experimental import pallas as pl
from jax.experimental.pallas import tpu as pltpu
from jax.sharding import Mesh
from jax.sharding import PartitionSpec as P

norm_eps = 1e-06
masked_score = -1e30


def head_sums(values, head_dim):
    width = values.shape[1]
    row = lax.broadcasted_iota(jnp.int32, (width, width), 0) // head_dim
    column = lax.broadcasted_iota(jnp.int32, (width, width), 1) // head_dim
    ones = jnp.where(row == column, 1.0, 0.0).astype(jnp.bfloat16)
    total = None
    for _ in range(3):
        part = values.astype(jnp.bfloat16)
        values = values - part.astype(jnp.float32)
        term = jnp.dot(part, ones, preferred_element_type=jnp.float32)
        total = term if total is None else total + term
    return total


def half_turn(values, head_dim):
    half = head_dim // 2
    width = values.shape[1]
    lane = lax.broadcasted_iota(jnp.int32, values.shape, 1) % head_dim
    ahead = pltpu.roll(values, width - half, 1)
    behind = pltpu.roll(values, half, 1)
    return jnp.where(lane < half, ahead, behind)


def signed(sine, head_dim):
    lane = lax.broadcasted_iota(jnp.int32, sine.shape, 1) % head_dim
    return jnp.where(lane < head_dim // 2, -sine, sine)


def head_norm_rotate(values, gain, cosine, sine, head_dim):
    scale = lax.rsqrt(head_sums(values * values, head_dim) / head_dim + norm_eps)
    normed = values * scale * gain
    return normed * cosine + half_turn(normed, head_dim) * signed(sine, head_dim)


def head_norm_rotate_back(grad, values, gain, cosine, sine, head_dim):
    grad = grad * cosine - half_turn(grad * sine, head_dim) * signed(
        jnp.ones_like(sine), head_dim
    )
    scale = lax.rsqrt(head_sums(values * values, head_dim) / head_dim + norm_eps)
    weighted = grad * gain
    inner = head_sums(weighted * values, head_dim)
    back = scale * weighted - values * (scale * scale * scale) * inner / head_dim
    return back, grad * values * scale


def wide(table, count):
    return jnp.concatenate([table] * count, axis=1)


def fill_mask(pieces, row, base_ref, segq_ref, segk_ref, mask_ref):
    size = segq_ref.shape[1]
    seg_query = segq_ref[pl.ds(row, 1), :]
    query_at = base_ref[0] + lax.broadcasted_iota(jnp.int32, (size, size), 1)
    for piece in range(pieces):
        count = segk_ref.shape[0] // segq_ref.shape[0]
        line = segk_ref[pl.ds(row * count + base_ref[1 + piece] // size, 1), :]
        seg_key = jnp.broadcast_to(line, (size, size)).astype(jnp.float32).T
        key_at = base_ref[1 + piece] + lax.broadcasted_iota(jnp.int32, (size, size), 0)
        allowed = (key_at <= query_at) & (
            seg_key == jnp.broadcast_to(seg_query, (size, size)).astype(jnp.float32)
        )
        mask_ref[piece * size : (piece + 1) * size, :] = jnp.where(allowed, 0.0, masked_score)


def attend_kernel(pieces, heads_kv, grouping, base_ref, q_ref, segq_ref, segk_ref, *refs):
    kv_refs = refs[:pieces]
    out_ref, log_ref, q_heads, k_heads, v_heads, mask_ref = refs[pieces:]
    row, group = pl.program_id(0), pl.program_id(1)
    size, head_dim = segq_ref.shape[1], k_heads.shape[2]

    @pl.when(group == 0)
    def _():
        for head in range(heads_kv):
            for j in range(grouping):
                at = (head * grouping + j) * head_dim
                q_heads[head, j * size : (j + 1) * size, :] = q_ref[:, at : at + head_dim]
            for piece in range(pieces):
                rows = slice(piece * size, (piece + 1) * size)
                at = head * head_dim
                k_heads[head, rows, :] = kv_refs[piece][:, at : at + head_dim]
                at += heads_kv * head_dim
                v_heads[head, rows, :] = kv_refs[piece][:, at : at + head_dim]
        fill_mask(pieces, row, base_ref, segq_ref, segk_ref, mask_ref)

    together = grouping if pieces <= 8 else 1
    turned = []
    for first in range(0, grouping, together):
        rows = slice(first * size, (first + together) * size)
        scores = lax.dot_general(
            k_heads[group], q_heads[group, rows, :], NT, preferred_element_type=jnp.float32
        ) + wide(mask_ref[...], together)
        top = jnp.max(scores, axis=0, keepdims=True)
        probs = jnp.exp(scores - top)
        total = jnp.sum(probs, axis=0, keepdims=True)
        probs_b = (probs * (1.0 / total)).astype(jnp.bfloat16)
        mixed = lax.dot_general(
            v_heads[group], probs_b, (((0,), (0,)), ((), ())), preferred_element_type=jnp.float32
        )
        turned += [mixed[:, j * size : (j + 1) * size].T for j in range(together)]
        log_ref[:, rows] = top + jnp.log(total)
    out_ref[...] = jnp.concatenate(turned, axis=1).astype(jnp.bfloat16)


def attend_call(heads_kv, grouping, bases, query_b, seg_here, seg_all, kv_pieces):
    pieces = len(kv_pieces)
    rows, size = seg_here.shape
    head_dim = kv_pieces[0].shape[1] // (2 * heads_kv)
    block = grouping * head_dim
    width = heads_kv * block
    keys = pieces * size
    row_block = lambda w: pl.BlockSpec((size, w), lambda r, g: (r, 0))
    whole = lambda a: pl.BlockSpec(a.shape, lambda r, g: (0,) * a.ndim)
    low, full = jnp.bfloat16, jnp.float32
    return pl.pallas_call(
        functools.partial(attend_kernel, pieces, heads_kv, grouping),
        grid=(rows, heads_kv),
        out_shape=[
            jax.ShapeDtypeStruct((rows * size, width), low),
            jax.ShapeDtypeStruct((rows, heads_kv, 1, grouping * size), full),
        ],
        in_specs=[
            pl.BlockSpec(memory_space=pltpu.SMEM),
            row_block(width),
            whole(seg_here),
            whole(seg_all),
        ]
        + [row_block(2 * heads_kv * head_dim)] * pieces,
        out_specs=[
            pl.BlockSpec((size, block), lambda r, g: (r, g)),
            pl.BlockSpec((None, None, 1, grouping * size), lambda r, g: (r, g, 0, 0)),
        ],
        scratch_shapes=[
            pltpu.VMEM((heads_kv, grouping * size, head_dim), low),
            pltpu.VMEM((heads_kv, keys, head_dim), low),
            pltpu.VMEM((heads_kv, keys, head_dim), low),
            pltpu.VMEM((keys, size), full),
        ],
        compiler_params=pltpu.CompilerParams(vmem_limit_bytes=60 * 1024 * 1024),
        cost_estimate=pl.CostEstimate(
            flops=4 * rows * size * keys * width * 4,
            bytes_accessed=4 * rows * size * width + 4 * rows * keys * heads_kv * head_dim,
            transcendentals=rows * heads_kv * grouping * size * keys,
        ),
    )(bases, query_b, seg_here, seg_all, *kv_pieces)


def attend_back_kernel(
    row,
    pieces,
    heads_kv,
    grouping,
    base_ref,
    q_ref,
    do_ref,
    segq_ref,
    segk_ref,
    log_ref,
    pre_ref,
    gain_ref,
    cos_ref,
    sin_ref,
    *refs,
):
    kv_refs = refs[:pieces]
    dq_ref, gain_rows_ref = refs[pieces : pieces + 2]
    dkv_refs = refs[pieces + 2 : 2 * pieces + 2]
    q_heads, do_heads, k_heads, v_heads, dk_heads, dv_heads, mask_ref = refs[2 * pieces + 2 :]
    group = pl.program_id(0)
    size, head_dim = segq_ref.shape[1], k_heads.shape[2]

    @pl.when(group == 0)
    def _():
        for head in range(heads_kv):
            for j in range(grouping):
                at = (head * grouping + j) * head_dim
                q_heads[head, j * size : (j + 1) * size, :] = q_ref[:, at : at + head_dim]
                do_heads[head, j * size : (j + 1) * size, :] = do_ref[:, at : at + head_dim]
            for piece in range(pieces):
                rows = slice(piece * size, (piece + 1) * size)
                at = head * head_dim
                k_heads[head, rows, :] = kv_refs[piece][:, at : at + head_dim]
                at += heads_kv * head_dim
                v_heads[head, rows, :] = kv_refs[piece][:, at : at + head_dim]
        fill_mask(pieces, row, base_ref, segq_ref, segk_ref, mask_ref)

    together = grouping if pieces <= 8 else 1
    turned = []
    for first in range(0, grouping, together):
        rows = slice(first * size, (first + together) * size)
        queries, grads = q_heads[group, rows, :], do_heads[group, rows, :]
        scores = lax.dot_general(
            k_heads[group], queries, NT, preferred_element_type=jnp.float32
        ) + wide(mask_ref[...], together)
        probs = jnp.exp(scores - log_ref[:, rows])
        grad_probs = lax.dot_general(
            v_heads[group], grads, NT, preferred_element_type=jnp.float32
        )
        grad_values = jnp.dot(
            probs.astype(jnp.bfloat16), grads, preferred_element_type=jnp.float32
        )
        delta = jnp.sum(probs * grad_probs, axis=0, keepdims=True)
        grad_scores = (probs * (grad_probs - delta)).astype(jnp.bfloat16)
        grad_keys = jnp.dot(grad_scores, queries, preferred_element_type=jnp.float32)
        if first:
            grad_values = grad_values + dv_heads[group].astype(jnp.float32)
            grad_keys = grad_keys + dk_heads[group].astype(jnp.float32)
        dv_heads[group] = grad_values.astype(dv_heads.dtype)
        dk_heads[group] = grad_keys.astype(dk_heads.dtype)
        mixed = lax.dot_general(
            k_heads[group], grad_scores, (((0,), (0,)), ((), ())), preferred_element_type=jnp.float32
        ) * (head_dim**-0.5)
        turned += [mixed[:, j * size : (j + 1) * size].T for j in range(together)]
    grad_query = jnp.concatenate(turned, axis=1)
    copies = grad_query.shape[1] // cos_ref.shape[1]
    back, gain_rows = head_norm_rotate_back(
        grad_query,
        pre_ref[...],
        gain_ref[...],
        wide(cos_ref[...], copies),
        wide(sin_ref[...], copies),
        head_dim,
    )
    dq_ref[...] = back.astype(jnp.bfloat16)
    gain_rows_ref[...] = jnp.sum(gain_rows, axis=0, keepdims=True)

    @pl.when(group == heads_kv - 1)
    def _():
        for piece in range(pieces):
            rows = slice(piece * size, (piece + 1) * size)
            dkv_refs[piece][...] = jnp.concatenate(
                [dk_heads[head, rows, :] for head in range(heads_kv)]
                + [dv_heads[head, rows, :] for head in range(heads_kv)],
                axis=1,
            )


def attend_back_call(
    row, heads_kv, grouping, bases, query_b, grad_att, seg_here, seg_all, logs, query_pre, gain, cosine, sine, kv_pieces
):
    pieces = len(kv_pieces)
    rows, size = seg_here.shape
    head_dim = kv_pieces[0].shape[1] // (2 * heads_kv)
    block = grouping * head_dim
    width = heads_kv * block
    keys = pieces * size
    kv_width = 2 * heads_kv * head_dim
    row_block = lambda w: pl.BlockSpec((size, w), lambda g: (row, 0))
    whole = lambda a: pl.BlockSpec(a.shape, lambda g: (0,) * a.ndim)
    low, full = jnp.bfloat16, jnp.float32
    heads = lambda n, t: pltpu.VMEM((heads_kv, n, head_dim), t)
    return pl.pallas_call(
        functools.partial(attend_back_kernel, row, pieces, heads_kv, grouping),
        grid=(heads_kv,),
        out_shape=[
            jax.ShapeDtypeStruct((size, width), low),
            jax.ShapeDtypeStruct((heads_kv, 1, block), full),
        ]
        + [jax.ShapeDtypeStruct((size, kv_width), low)] * pieces,
        in_specs=[
            pl.BlockSpec(memory_space=pltpu.SMEM),
            row_block(width),
            row_block(width),
            whole(seg_here),
            whole(seg_all),
            pl.BlockSpec((None, None, 1, grouping * size), lambda g: (row, g, 0, 0)),
            pl.BlockSpec((size, block), lambda g: (row, g)),
            whole(gain),
            row_block(cosine.shape[1]),
            row_block(sine.shape[1]),
        ]
        + [row_block(kv_width)] * pieces,
        out_specs=[
            pl.BlockSpec((size, block), lambda g: (0, g)),
            pl.BlockSpec((None, 1, block), lambda g: (g, 0, 0)),
        ]
        + [pl.BlockSpec((size, kv_width), lambda g: (0, 0))] * pieces,
        scratch_shapes=[
            heads(grouping * size, low),
            heads(grouping * size, low),
            heads(keys, low),
            heads(keys, low),
            heads(keys, low),
            heads(keys, low),
            pltpu.VMEM((keys, size), full),
        ],
        compiler_params=pltpu.CompilerParams(vmem_limit_bytes=60 * 1024 * 1024),
        cost_estimate=pl.CostEstimate(
            flops=10 * size * keys * width * 4,
            bytes_accessed=8 * size * width + 8 * keys * heads_kv * head_dim,
            transcendentals=heads_kv * grouping * size * keys,
        ),
    )(bases, query_b, grad_att, seg_here, seg_all, logs, query_pre, gain, cosine, sine, *kv_pieces)


def place_copies(spots, pieces, place_ref, w_ref, sems):
    x_at, core_at, z_at, y_at = [place_ref[i] for i in range(4)]
    copies = []
    for index, (dx, dy, dc, column) in enumerate(spots):
        piece = pieces[index]
        planes, size, width = piece.shape
        for t in range(planes):
            row = (x_at + dx - 2 * x_at * dx) * 2 + (core_at + dc - 2 * core_at * dc)
            row = (row * planes + lax.rem(z_at + t, planes)) * 2 + (y_at + dy - 2 * y_at * dy)
            start = pl.multiple_of(row * size, size)
            copies.append(
                pltpu.make_async_copy(
                    piece.at[t],
                    w_ref.at[pl.ds(start, size), column : column + width],
                    sems.at[index, t],
                )
            )
    return copies


def project_kernel(width_q, head_dim, spots, place_ref, x_ref, gain_ref, gq_ref, gk_ref, cos_ref, sin_ref, *refs):
    pieces, outs, (w_ref, sems) = refs[: len(spots)], refs[len(spots) : -2], refs[-2:]
    copies_in = place_copies(spots, pieces, place_ref, w_ref, sems)
    for copy in copies_in:
        copy.start()
    normed_ref, pre_ref, kpre_ref, q_ref, kv_ref = outs
    values = x_ref[...].astype(jnp.float32)
    scale = lax.rsqrt(jnp.mean(values * values, axis=1, keepdims=True) + norm_eps)
    normed_ref[...] = (values * scale * gain_ref[...]).astype(jnp.bfloat16)
    block = 256
    cosine, sine = cos_ref[...], sin_ref[...]
    for copy in copies_in:
        copy.wait()
    total = w_ref.shape[1]
    for first in range(0, width_q, block):
        pre = jnp.dot(
            normed_ref[...], w_ref[:, first : first + block], preferred_element_type=jnp.float32
        )
        pre_ref[:, first : first + block] = pre
        copies = block // cosine.shape[1]
        rotated = head_norm_rotate(
            pre, gq_ref[...], wide(cosine, copies), wide(sine, copies), head_dim
        )
        q_ref[:, first : first + block] = (rotated * (head_dim**-0.5)).astype(jnp.bfloat16)
    pre = jnp.dot(normed_ref[...], w_ref[:, width_q:], preferred_element_type=jnp.float32)
    kpre_ref[...] = pre
    copies = pre.shape[1] // cosine.shape[1]
    rotated = head_norm_rotate(pre, gk_ref[...], wide(cosine, copies), wide(sine, copies), head_dim)
    lane = lax.broadcasted_iota(jnp.int32, pre.shape, 1)
    kv_ref[...] = jnp.where(lane < pre.shape[1] // 2, rotated, pre).astype(jnp.bfloat16)


def project_call(width_q, head_dim, total, place, x, gain, gain_q, gain_k, cosine, sine, spots, pieces):
    tokens, features = x.shape
    kv = total - width_q
    low, full = jnp.bfloat16, jnp.float32
    vm = pl.BlockSpec(memory_space=pltpu.VMEM)
    return pl.pallas_call(
        functools.partial(project_kernel, width_q, head_dim, spots),
        out_shape=[
            jax.ShapeDtypeStruct((tokens, features), low),
            jax.ShapeDtypeStruct((tokens, width_q), full),
            jax.ShapeDtypeStruct((tokens, kv), full),
            jax.ShapeDtypeStruct((tokens, width_q), low),
            jax.ShapeDtypeStruct((tokens, kv), low),
        ],
        in_specs=[pl.BlockSpec(memory_space=pltpu.SMEM)]
        + [vm] * 6
        + [pl.BlockSpec(memory_space=pl.ANY)] * len(pieces),
        out_specs=[vm] * 5,
        scratch_shapes=[
            pltpu.VMEM((features, total), low),
            pltpu.SemaphoreType.DMA((len(pieces), pieces[0].shape[0])),
        ],
        compiler_params=pltpu.CompilerParams(vmem_limit_bytes=60 * 1024 * 1024),
        cost_estimate=pl.CostEstimate(
            flops=2 * tokens * features * total,
            bytes_accessed=2 * features * total + 10 * tokens * features,
            transcendentals=tokens,
        ),
    )(place, x, gain, gain_q, gain_k, cosine, sine, *pieces)


def keys_back_kernel(head_dim, grad_ref, kpre_ref, gk_ref, cos_ref, sin_ref, out_ref, gain_rows_ref):
    grad = grad_ref[...]
    copies = grad.shape[1] // cos_ref.shape[1]
    back, gain_rows = head_norm_rotate_back(
        grad,
        kpre_ref[...],
        gk_ref[...],
        wide(cos_ref[...], copies),
        wide(sin_ref[...], copies),
        head_dim,
    )
    lane = lax.broadcasted_iota(jnp.int32, grad.shape, 1)
    out_ref[...] = jnp.where(lane < grad.shape[1] // 2, back, grad).astype(jnp.bfloat16)
    gain_rows_ref[...] = jnp.sum(gain_rows, axis=0, keepdims=True)


def keys_back_call(head_dim, grad, kpre, gain_k, cosine, sine):
    vm = pl.BlockSpec(memory_space=pltpu.VMEM)
    return pl.pallas_call(
        functools.partial(keys_back_kernel, head_dim),
        out_shape=[
            jax.ShapeDtypeStruct(grad.shape, jnp.bfloat16),
            jax.ShapeDtypeStruct((1, grad.shape[1]), jnp.float32),
        ],
        in_specs=[vm] * 5,
        out_specs=[vm] * 2,
        compiler_params=pltpu.CompilerParams(vmem_limit_bytes=60 * 1024 * 1024),
    )(grad, kpre, gain_k, cosine, sine)


def input_kernel(spots, place_ref, g_ref, x_ref, gain_ref, mid_ref, *refs):
    pieces = refs[: len(spots)]
    out_ref, gain_rows_ref, w_ref, sems = refs[len(spots) :]
    copies = place_copies(spots, pieces, place_ref, w_ref, sems)
    for copy in copies:
        copy.start()
    values = x_ref[...].astype(jnp.float32)
    scale = lax.rsqrt(jnp.mean(values * values, axis=1, keepdims=True) + norm_eps)
    for copy in copies:
        copy.wait()
    grad = lax.dot_general(
        g_ref[...], w_ref[...], (((1,), (1,)), ((), ())), preferred_element_type=jnp.float32
    )
    weighted = grad * gain_ref[...]
    inner = jnp.sum(weighted * values, axis=1, keepdims=True)
    back = scale * weighted - values * (scale * scale * scale) * inner / values.shape[1]
    out_ref[...] = mid_ref[...] + back
    gain_rows_ref[...] = jnp.sum(grad * values * scale, axis=0, keepdims=True)


def input_call(place, grad_qkv, x, gain, grad_middle, spots, pieces):
    tokens, features = x.shape
    total = grad_qkv.shape[1]
    vm = pl.BlockSpec(memory_space=pltpu.VMEM)
    return pl.pallas_call(
        functools.partial(input_kernel, spots),
        out_shape=[
            jax.ShapeDtypeStruct((tokens, features), jnp.float32),
            jax.ShapeDtypeStruct((1, features), jnp.float32),
        ],
        in_specs=[pl.BlockSpec(memory_space=pltpu.SMEM)]
        + [vm] * 4
        + [pl.BlockSpec(memory_space=pl.ANY)] * len(pieces),
        out_specs=[vm] * 2,
        scratch_shapes=[
            pltpu.VMEM((features, total), jnp.bfloat16),
            pltpu.SemaphoreType.DMA((len(pieces), pieces[0].shape[0])),
        ],
        compiler_params=pltpu.CompilerParams(vmem_limit_bytes=60 * 1024 * 1024),
        cost_estimate=pl.CostEstimate(
            flops=2 * tokens * features * total,
            bytes_accessed=2 * features * total + 10 * tokens * features,
            transcendentals=tokens,
        ),
    )(place, grad_qkv, x, gain, grad_middle, *pieces)

ANY = pl.BlockSpec(memory_space=pl.ANY)
VMEM = pl.BlockSpec(memory_space=pltpu.VMEM)
SMEM = pl.BlockSpec(memory_space=pltpu.SMEM)
NT = (((1,), (1,)), ((), ()))


def params():
    return pltpu.CompilerParams(vmem_limit_bytes=60 * 1024 * 1024)


def cuts(total, step):
    edges = list(range(0, total - step // 2, step)) + [total]
    return list(zip(edges[:-1], edges[1:]))


def weight_copies(planes, gathered, which, target, sems):
    size = gathered.shape[2]
    return [
        pltpu.make_async_copy(
            gathered.at[core * planes + z, which],
            target.at[pl.ds((2 * z + core) * size, size)],
            sems.at[core * planes + z],
        )
        for core in range(2)
        for z in range(planes)
    ]


def ffn_kernel(planes, blocks, chained, place_ref, *refs):
    refs = list(refs)
    take = lambda n: [refs.pop(0) for _ in range(n)]
    x_refs, c_refs = take(blocks), take(blocks)
    before = take(blocks) if chained else None
    (gathered,) = take(1)
    outs = take(4 * blocks)
    weights, sems = refs
    copies = [
        weight_copies(planes, gathered, which, weights.at[which], sems.at[which])
        for which in range(3)
    ]
    for group in copies:
        for copy in group:
            copy.start()
    waiting = list(copies)

    def arrive():
        if waiting:
            for copy in waiting.pop(0):
                copy.wait()

    features, units = weights.shape[1:]
    for block in range(blocks):
        hidden_ref, dgate_ref, dup_ref, dx_ref = outs[4 * block : 4 * block + 4]
        for first, last in cuts(units, 512):
            arrive()
            gate = jnp.dot(
                x_refs[block][...], weights[0, :, first:last], preferred_element_type=jnp.float32
            )
            arrive()
            up = jnp.dot(
                x_refs[block][...], weights[1, :, first:last], preferred_element_type=jnp.float32
            )
            arrive()
            dh = jnp.dot(
                c_refs[block][...], weights[2, :, first:last], preferred_element_type=jnp.float32
            )
            sigma = 1.0 / (1.0 + jnp.exp(-gate))
            silu = gate * sigma
            hidden_ref[:, first:last] = (silu * up).astype(jnp.bfloat16)
            dup_ref[:, first:last] = (dh * silu).astype(jnp.bfloat16)
            dgate_ref[:, first:last] = (dh * up * (sigma + silu * (1.0 - sigma))).astype(
                jnp.bfloat16
            )
        for first, last in cuts(features, 512):
            dx = lax.dot_general(
                dgate_ref[...], weights[0, first:last], NT, preferred_element_type=jnp.float32
            ) + lax.dot_general(
                dup_ref[...], weights[1, first:last], NT, preferred_element_type=jnp.float32
            )
            if chained:
                dx = dx + before[block][:, first:last].astype(jnp.float32)
            dx_ref[:, first:last] = dx.astype(jnp.bfloat16)


def ffn_call(planes, place, xs, cs, gathered, before=None):
    blocks = len(xs)
    tokens, features = xs[0].shape
    units = gathered.shape[3]
    low = jnp.bfloat16
    one = [jax.ShapeDtypeStruct((tokens, units), low)] * 3 + [
        jax.ShapeDtypeStruct((tokens, features), low)
    ]
    chained = before is not None
    operands = [*xs, *cs, *(before or [])]
    return pl.pallas_call(
        functools.partial(ffn_kernel, planes, blocks, chained),
        out_shape=one * blocks,
        in_specs=[SMEM] + [VMEM] * len(operands) + [ANY],
        out_specs=[VMEM] * (4 * blocks),
        scratch_shapes=[
            pltpu.VMEM((3, features, units), low),
            pltpu.SemaphoreType.DMA((3, 2 * planes)),
        ],
        compiler_params=params(),
        cost_estimate=pl.CostEstimate(
            flops=10 * blocks * tokens * features * units,
            bytes_accessed=6 * features * units + 8 * blocks * tokens * features,
            transcendentals=blocks * tokens * units,
        ),
    )(place, *operands, gathered)


def weight_grad_kernel(blocks, place_ref, *refs):
    a_refs = [refs[:blocks], refs[blocks : 2 * blocks]]
    b_refs = [refs[(2 + i) * blocks : (3 + i) * blocks] for i in range(3)]
    own_ref, other_ref, turned = refs[5 * blocks :]
    size, units = own_ref.shape[1:]
    tokens = a_refs[0][0].shape[0]
    core_at = place_ref[1]
    for kind in range(2):
        for block in range(blocks):
            turned[kind, :, block * tokens : (block + 1) * tokens] = a_refs[kind][block][...].T
    for out_ref, half in ((other_ref, 1 - core_at), (own_ref, core_at)):
        rows = pl.ds(pl.multiple_of(half * size, size), size)
        for which in range(3):
            for first, last in cuts(units, 512):
                total = None
                for block in range(blocks):
                    part = jnp.dot(
                        turned[which // 2, rows, block * tokens : (block + 1) * tokens],
                        b_refs[which][block][:, first:last],
                        preferred_element_type=jnp.float32,
                    )
                    total = part if total is None else total + part
                out_ref[which, :, first:last] = total.astype(jnp.bfloat16)


def weight_grad_call(planes, place, xs, cs, dgates, dups, hiddens):
    blocks = len(xs)
    tokens, features = xs[0].shape
    units = dgates[0].shape[1]
    size = features // (2 * planes)
    out = jax.ShapeDtypeStruct((planes, 3, size, units), jnp.bfloat16)
    column = pl.BlockSpec((tokens, 2 * size), lambda t, place: (0, t))
    return pl.pallas_call(
        functools.partial(weight_grad_kernel, blocks),
        out_shape=[out, out],
        grid_spec=pltpu.PrefetchScalarGridSpec(
            num_scalar_prefetch=1,
            grid=(planes,),
            in_specs=[column] * (2 * blocks)
            + [pl.BlockSpec((tokens, units), lambda t, place: (0, 0))] * (3 * blocks),
            out_specs=[pl.BlockSpec((None, 3, size, units), lambda t, place: (t, 0, 0, 0))] * 2,
            scratch_shapes=[pltpu.VMEM((2, 2 * size, blocks * tokens), jnp.bfloat16)],
        ),
        compiler_params=params(),
        cost_estimate=pl.CostEstimate(
            flops=6 * blocks * tokens * features * units,
            bytes_accessed=6 * blocks * tokens * units + 6 * features * units,
            transcendentals=0,
        ),
    )(place, *xs, *cs, *dgates, *dups, *hiddens)


def down_kernel(planes, blocks, parts, place_ref, *refs):
    refs = list(refs)
    take = lambda n: [refs.pop(0) for _ in range(n)]
    h_refs = [take(blocks) for _ in range(parts)]
    gathered = take(parts)
    outs = take(blocks)
    weights = take(parts)
    (sems,) = refs
    copies = []
    for part in range(parts):
        copies += weight_copies(planes, gathered[part], 2, weights[part], sems.at[part])
    for copy in copies:
        copy.start()
    for copy in copies:
        copy.wait()
    for block in range(blocks):
        for first, last in cuts(weights[0].shape[0], 512):
            total = None
            for part in range(parts):
                term = lax.dot_general(
                    h_refs[part][block][...],
                    weights[part][first:last],
                    NT,
                    preferred_element_type=jnp.float32,
                )
                total = term if total is None else total + term
            outs[block][:, first:last] = total.astype(jnp.bfloat16)


def down_call(planes, place, hidden_parts, gathered_parts):
    parts, blocks = len(hidden_parts), len(hidden_parts[0])
    tokens = hidden_parts[0][0].shape[0]
    size = gathered_parts[0].shape[2]
    features = 2 * planes * size
    units = [h[0].shape[1] for h in hidden_parts]
    return pl.pallas_call(
        functools.partial(down_kernel, planes, blocks, parts),
        out_shape=[jax.ShapeDtypeStruct((tokens, features), jnp.bfloat16)] * blocks,
        in_specs=[SMEM] + [VMEM] * (parts * blocks) + [ANY] * parts,
        out_specs=[VMEM] * blocks,
        scratch_shapes=[pltpu.VMEM((features, n), jnp.bfloat16) for n in units]
        + [pltpu.SemaphoreType.DMA((parts, 2 * planes))],
        compiler_params=params(),
        cost_estimate=pl.CostEstimate(
            flops=2 * blocks * tokens * features * sum(units),
            bytes_accessed=2 * features * sum(units) + 8 * blocks * tokens * features,
            transcendentals=0,
        ),
    )(
        place,
        *[h for part in hidden_parts for h in part],
        *gathered_parts,
    )


def rms_apply(values, gain_vec):
    row_scale = lax.rsqrt(jnp.mean(values * values, axis=-1, keepdims=True) + norm_eps)
    return values * row_scale * gain_vec


def rms_back(values, gain_vec, grad_in):
    row_scale = lax.rsqrt(jnp.mean(values * values, axis=-1, keepdims=True) + norm_eps)
    weighted = grad_in * gain_vec
    inner_sum = jnp.sum(weighted * values, axis=-1, keepdims=True)
    grad_values = (
        row_scale * weighted
        - values * (row_scale * row_scale * row_scale) * inner_sum / values.shape[-1]
    )
    return (grad_values, grad_in * values * row_scale)


def rotary_tables(positions, head_dim):
    half_dim = head_dim // 2
    frequencies = 10000.0 ** (-2.0 * jnp.arange(half_dim).astype(jnp.float32) / head_dim)
    angles = positions.astype(jnp.float32)[..., None] * frequencies
    angles = jnp.concatenate([angles, angles], axis=-1)
    return (jnp.cos(angles), jnp.sin(angles))


def times_transposed(left, right):
    return lax.dot_general(
        left, right, (((1,), (1,)), ((), ())), preferred_element_type=jnp.float32
    )


def transposed_times(left, right):
    return lax.dot_general(
        left, right, (((0,), (0,)), ((), ())), preferred_element_type=jnp.float32
    )


def swap(values, axis_name, bit):
    count = lax.axis_size(axis_name)
    return lax.ppermute(values, axis_name, [(i, i ^ bit) for i in range(count)])


def ring(values, shift):
    count = lax.axis_size("z")
    return lax.ppermute(values, "z", [(i, (i + shift) % count) for i in range(count)])


def core_swap(values):
    return swap(values, "core", 1)


def x_swap(values):
    return swap(values, "x", 1)


def y_swap(values):
    return swap(values, "y", 1)


def sum_over(values, names):
    for axis_name in names:
        bit = 1
        while bit < lax.axis_size(axis_name):
            values = values + swap(values, axis_name, bit)
            bit *= 2
    return values


def places():
    return tuple(lax.axis_index(name) for name in ("x", "core", "z", "y"))


def in_order(first, other, bit, axis):
    return jnp.where(
        bit == 0, jnp.stack([first, other], axis=axis), jnp.stack([other, first], axis=axis)
    )


def corner(values):
    moved = lax.ppermute(values, ("core", "y"), [(1, 2), (2, 1)])
    return jnp.where(lax.axis_index("core") == lax.axis_index("y"), values, moved)


def chain(values, shift):
    count = lax.axis_size("z")
    moves = [(i, i + shift) for i in range(count) if 0 <= i + shift < count]
    return lax.ppermute(values, "z", moves)


def hold(values, *others):
    return lax.optimization_barrier((values, *others))[0]


def together(*values):
    return lax.optimization_barrier(values)


def ring_gather(values):
    pieces = [values]
    for _ in range(lax.axis_size("z") - 1):
        pieces.append(ring(pieces[-1], -1))
    return pieces


def direct_gather(values):
    return [values] + [ring(values, -t) for t in range(1, lax.axis_size("z"))]


def ring_scatter(pieces):
    count = len(pieces)
    moving = None
    for step in range(1, count):
        block = pieces[count - step]
        if moving is not None:
            block = (block.astype(jnp.float32) + moving.astype(jnp.float32)).astype(jnp.bfloat16)
        moving = ring(block, 1)
    return pieces[0].astype(jnp.float32) + moving.astype(jnp.float32)


def turn(values, start):
    count = values.shape[0]
    return lax.dynamic_slice_in_dim(jnp.concatenate([values, values], axis=0), start, count, 0)


def turn_columns(values, start, width):
    return lax.dynamic_slice_in_dim(
        jnp.concatenate([values, values], axis=1), start * width, values.shape[1], 1
    )


def pick(values, bit, axis):
    return (
        lax.dynamic_index_in_dim(values, bit, axis, keepdims=False),
        lax.dynamic_index_in_dim(values, 1 - bit, axis, keepdims=False),
    )


def add_low(left, right):
    return (left.astype(jnp.float32) + right.astype(jnp.float32)).astype(jnp.bfloat16)


def gather_tokens(values):
    half = values.shape[1] // 2
    from_x = x_swap(values)
    from_y = y_swap(values)
    from_xy = jnp.concatenate([y_swap(from_x[:, :half]), x_swap(from_y[:, half:])], axis=1)
    return [values, from_x, from_y, from_xy]


def scatter_corner(blocks):
    half = blocks[3].shape[1] // 2
    return x_swap(blocks[3][:, :half]), y_swap(blocks[3][:, half:])


def scatter_sides(blocks, via_x, via_y):
    _, to_x, to_y, _ = blocks
    half = to_x.shape[1] // 2
    to_y = jnp.concatenate([add_low(to_y[:, :half], via_x), to_y[:, half:]], axis=1)
    to_x = jnp.concatenate([to_x[:, :half], add_low(to_x[:, half:], via_y)], axis=1)
    return x_swap(to_x), y_swap(to_y)


def scatter_total(blocks, from_x, from_y):
    return (
        blocks[0].astype(jnp.float32) + from_x.astype(jnp.float32) + from_y.astype(jnp.float32)
    )


def local(
    inputs,
    cotangent,
    positions,
    segment_ids,
    w_query,
    w_key,
    w_value,
    w_out,
    w_gate,
    w_up,
    w_down,
    gain_attn,
    gain_query,
    gain_key,
    gain_ffn,
):
    rows_here, seg_tok, feature_count = inputs.shape
    tokens_here = rows_here * seg_tok
    head_dim = gain_query.shape[0]
    heads_query = w_query.shape[1] // head_dim
    heads_kv = w_key.shape[1] // head_dim
    grouping = heads_query // heads_kv
    planes = lax.axis_size("z")
    rows_count, seq_count = 4, 2 * planes
    row_len = seg_tok * seq_count
    x_at, core_at, z_at, y_at = places()
    seq_place = 2 * z_at + y_at
    row_place = 2 * x_at + core_at
    device = row_place * seq_count + seq_place
    place = jnp.stack([x_at, core_at, z_at, y_at]).astype(jnp.int32)
    gain_size = gain_attn.shape[0]
    width_q, width_k = w_query.shape[1], w_key.shape[1]
    low = jnp.bfloat16

    shared = jnp.zeros((2 * feature_count + rows_count * rows_here * row_len,), jnp.float32)

    def put(shared, values, start):
        return lax.dynamic_update_slice_in_dim(shared, values.astype(jnp.float32), start, 0)

    shared = put(shared, gain_attn, device * gain_size)
    shared = put(shared, gain_ffn, feature_count + device * gain_size)
    for row in range(rows_here):
        start = ((row_place * rows_here + row) * seq_count + seq_place) * seg_tok
        shared = put(shared, segment_ids[row], 2 * feature_count + start)
    cotangent_here = cotangent.reshape(tokens_here, feature_count)
    shared = sum_over(shared.reshape(-1, 128), ("core", "z"))
    qkv_here = jnp.concatenate([w_query, w_key, w_value], axis=1)
    qkv_own, shared = together(
        jnp.stack(direct_gather(qkv_here)), sum_over(shared, ("x", "y"))
    )
    shared = shared.reshape(-1)
    attn_gain = shared[:feature_count].reshape(1, -1)
    ffn_gain = shared[feature_count : 2 * feature_count].reshape(1, -1)
    seg_all = shared[2 * feature_count :].reshape(rows_count, rows_here * seq_count, seg_tok)
    seg_all = lax.dynamic_index_in_dim(seg_all, row_place, 0, keepdims=False)
    seg_here = segment_ids.astype(jnp.float32)

    qkv_width = qkv_own.shape[2]
    cut = 512
    out_own = turn(jnp.stack(direct_gather(hold(w_out, qkv_own))), (planes - z_at) % planes)
    qkv_x, qkv_y = together(x_swap(qkv_own), y_swap(qkv_own))
    down_turned = w_down.T
    ffn_width = w_gate.shape[1]
    ffn_cut = (ffn_width // 256 + 1) * 128
    stacks = [
        jnp.stack([w[:, first:last] for w in (w_gate, w_up, down_turned)])
        for first, last in ((0, ffn_cut), (ffn_cut, ffn_width))
    ]
    qkv_a, qkv_b, out_own, first_stack = together(
        y_swap(qkv_x[..., :cut]),
        x_swap(qkv_y[..., cut:]),
        out_own,
        corner(hold(stacks[0], qkv_x)),
    )
    qkv_pieces = [qkv_own, qkv_x, qkv_y, qkv_a, qkv_b]
    qkv_pieces += [core_swap(piece) for piece in qkv_pieces]
    spots = [(0, 0, 0, 0), (1, 0, 0, 0), (0, 1, 0, 0), (1, 1, 0, 0), (1, 1, 0, cut)]
    spots = tuple(spots + [(dx, dy, 1, column) for dx, dy, _, column in spots])
    gathered_first = lax.all_gather(first_stack, ("core", "z"), axis=0)

    inputs_here = inputs.reshape(tokens_here, feature_count)
    cosine, sine = rotary_tables(positions.reshape(tokens_here), head_dim)
    cosine = jnp.concatenate([cosine, cosine], axis=1)
    sine = jnp.concatenate([sine, sine], axis=1)
    gain_q = jnp.tile(gain_query.astype(jnp.float32), grouping).reshape(1, -1)
    gain_k = jnp.tile(gain_key.astype(jnp.float32), 2 * heads_kv).reshape(1, -1)
    normed, query_pre, kv_pre, query_b, kv_here = project_call(
        width_q, head_dim, qkv_width, place, inputs_here, attn_gain, gain_q, gain_k, cosine, sine,
        spots, qkv_pieces,
    )

    cot_own = hold(cotangent_here, kv_here)
    *kv_far, near, out_y, cot_x, cot_y = together(
        *[chain(kv_here, t) for t in range(1, planes)],
        y_swap(kv_here),
        y_swap(hold(out_own, kv_here)),
        x_swap(cot_own),
        y_swap(cot_own),
    )
    out_block = in_order(out_own, out_y, y_at, 1)
    kv_own = [kv_here] + list(kv_far)
    *kv_other, out_x = together(*[y_swap(piece) for piece in kv_far], x_swap(out_block))
    cot_xy = x_swap(hold(cot_y, out_x))
    kv_other = [near] + list(kv_other)
    out_block = in_order(out_block, out_x, x_at, 0)
    kv_pieces, bases = [], [seq_place * seg_tok]
    for t in range(planes):
        for dy, piece in enumerate((kv_own[t], kv_other[t])):
            kv_pieces.append(piece)
            bases.append(((z_at - t + planes) % planes * 2 + (y_at + dy) % 2) * seg_tok)
    bases = jnp.stack(bases).astype(jnp.int32)
    attended_b, logs = attend_call(
        heads_kv, grouping, bases, query_b, seg_here, seg_all, kv_pieces
    )
    attended_b, out_core, second_stack, cot_xy = together(
        attended_b, core_swap(out_block), corner(hold(stacks[1], kv_other[-1])), cot_xy
    )
    cot_blocks = [cotangent_here, cot_x, cot_y, cot_xy]
    parts = [gathered_first, lax.all_gather(second_stack, ("core", "z"), axis=0)]
    out_full = in_order(out_block, out_core, core_at, 1).reshape(-1, feature_count)
    residual = inputs_here.astype(jnp.float32)
    middle = residual + jnp.dot(attended_b, out_full, preferred_element_type=jnp.float32)
    ffn_in = rms_apply(middle, ffn_gain).astype(low)
    ffn_blocks = gather_tokens(ffn_in)

    before, where = None, place
    hidden_parts, home, sums = [], [], []
    for gathered in parts:
        result = ffn_call(
            planes, where, ffn_blocks, cot_blocks, gathered, before
        )
        hiddens, dgates, dups, before = [result[i::4] for i in range(4)]
        hidden_parts.append(hiddens)
        own, other = weight_grad_call(
            planes, place, ffn_blocks, cot_blocks, dgates, dups, hiddens
        )
        both = add_low(own, core_swap(other))
        where = hold(place, both) if not sums else place
        sums.append(lax.psum_scatter(both, "z", scatter_dimension=0))
    via_x, via_y, last_own = together(*scatter_corner(before), own)
    from_x, from_y, both, *down_blocks = together(
        *scatter_sides(before, via_x, via_y),
        both,
        *down_call(planes, hold(place, last_own), hidden_parts, parts),
    )
    grad_ffn_in = scatter_total(before, from_x, from_y)
    grad_mid_ffn, gain_ffn_rows = rms_back(middle, ffn_gain, grad_ffn_in)
    grad_middle = cotangent_here.astype(jnp.float32) + grad_mid_ffn
    grad_gain_ffn = jnp.sum(gain_ffn_rows, axis=0)
    grad_branch = grad_middle.astype(low)
    grad_attended = times_transposed(grad_branch, out_full).astype(low)

    def over_core(grad):
        keep, send = pick(grad.reshape(2, 2, planes, 2, -1, grad.shape[1]), core_at, 1)
        return add_low(keep, core_swap(send))

    def over_x(block):
        keep, send = pick(block, x_at, 0)
        return add_low(keep, x_swap(send))

    def over_y(block, axis):
        keep, send = pick(block, y_at, axis)
        return add_low(keep, y_swap(send))

    def over_z(block):
        block = turn(block, z_at)
        total = block[0].astype(jnp.float32)
        for t in range(1, planes):
            total = total + ring(block[t], t).astype(jnp.float32)
        return total

    def back(row, bases):
        result = attend_back_call(
            row, heads_kv, grouping, bases, query_b, grad_attended, seg_here, seg_all, logs,
            query_pre, gain_q, cosine, sine, kv_pieces,
        )
        return result[0], result[1], result[2:]

    def over_pairs(dkv):
        return [add_low(dkv[2 * t], y_swap(dkv[2 * t + 1])) for t in range(planes)]

    def over_planes(pairs):
        return [pairs[0]] + [chain(pairs[t], -t) for t in range(1, planes)]

    grad_rows, gain_rows, pairs = [], [], []
    for row in range(rows_here):
        start = bases if row == 0 else hold(bases, grad_rows[-1])
        grad_row, gain_row, dkv = back(row, start)
        if row == 0:
            via_x, via_y, grad_row = together(*scatter_corner(down_blocks), grad_row)
        if row == 1:
            from_x, from_y, out_core, grad_row, *pairs[0] = together(
                *scatter_sides(down_blocks, via_x, via_y),
                over_core(
                    transposed_times(hold(attended_b, grad_rows[0]), grad_branch).astype(low)
                ),
                grad_row,
                *pairs[0],
            )
        grad_rows.append(grad_row)
        gain_rows.append(gain_row)
        pairs.append(over_pairs(dkv))
    down_mine = scatter_total(down_blocks, from_x, from_y)
    grad_query_b = jnp.concatenate(grad_rows, axis=0)
    gain_q_rows = jnp.stack(gain_rows)
    grad_query_w = transposed_times(normed, grad_query_b).astype(low)
    middle_q = width_q // 2
    *tied, query_a, query_b2, out_x, first_sum = together(
        *[piece for group in pairs[:-1] for piece in over_planes(group)],
        *pairs[-1],
        over_core(grad_query_w[:, :middle_q]),
        over_core(grad_query_w[:, middle_q:]),
        over_x(out_core),
        sums[0],
    )
    landed = [tied[i * planes : (i + 1) * planes] for i in range(rows_here)]
    *last, query_a, query_b2, out_y = together(
        *over_planes(landed[-1]), over_x(query_a), over_y(query_b2, 2), over_y(out_x, 1)
    )
    landed[-1] = last
    moving = []
    for pieces in landed:
        total = pieces[0].astype(jnp.float32)
        for piece in pieces[1:]:
            total = total + piece.astype(jnp.float32)
        moving.append(total)
    moving = jnp.concatenate(moving, axis=0)
    grad_kv_b, gain_k_rows = keys_back_call(head_dim, moving, kv_pre, gain_k, cosine, sine)
    kv_core, query_a, query_b2, grad_out_mine = together(
        over_core(transposed_times(normed, grad_kv_b).astype(low)),
        over_y(query_a, 1),
        over_x(query_b2),
        over_z(out_y),
    )
    grad_qkv_b = jnp.concatenate([grad_query_b, grad_kv_b], axis=1)
    grad_inputs, grad_gain_attn = input_call(
        hold(place, kv_core), grad_qkv_b, inputs_here, attn_gain, grad_middle, spots, qkv_pieces
    )
    kv_y, last_sum = together(over_y(kv_core, 2), sums[1])
    grad_kv_mine = over_z(over_x(kv_y))
    grad_query_mine = over_z(jnp.concatenate([query_a, query_b2], axis=2))
    home = [corner(mine).astype(jnp.float32) for mine in (first_sum, last_sum)]
    home = jnp.concatenate(home, axis=2)
    output_b = (middle + down_mine).astype(low).reshape(inputs.shape)
    gain_q_rows = jnp.sum(gain_q_rows.reshape(-1, head_dim), axis=0)
    gain_k_rows = jnp.sum(gain_k_rows.reshape(-1, head_dim)[:heads_kv], axis=0)
    small = jnp.concatenate([grad_gain_attn.reshape(-1), grad_gain_ffn, gain_q_rows, gain_k_rows])
    small = sum_over(small.reshape(-1, 128), ("x", "y", "core", "z")).reshape(-1)
    return (
        output_b,
        grad_inputs.reshape(inputs.shape),
        grad_query_mine,
        grad_kv_mine[:, :width_k],
        grad_kv_mine[:, width_k:],
        grad_out_mine,
        home[0],
        home[1],
        home[2].T,
        lax.dynamic_slice_in_dim(small, device * gain_size, gain_size),
        small[2 * feature_count : 2 * feature_count + head_dim],
        small[2 * feature_count + head_dim :],
        lax.dynamic_slice_in_dim(small, feature_count + device * gain_size, gain_size),
    )


def solution(mesh):
    rows, seq = mesh.devices.shape
    grid = Mesh(mesh.devices.reshape(2, rows // 2, seq // 2, 2), ("x", "core", "z", "y"))
    return jax.shard_map(
        local,
        mesh=grid,
        in_specs=(
            P(("x", "core"), ("z", "y"), None),
            P(("x", "core"), ("z", "y"), None),
            P(("x", "core"), ("z", "y")),
            P(("x", "core"), ("z", "y")),
            P(("x", "core", "z", "y"), None),
            P(("x", "core", "z", "y"), None),
            P(("x", "core", "z", "y"), None),
            P(("x", "core", "z", "y"), None),
            P(("z", "y"), ("x", "core")),
            P(("z", "y"), ("x", "core")),
            P(("x", "core"), ("z", "y")),
            P(("x", "core", "z", "y")),
            P(),
            P(),
            P(("x", "core", "z", "y")),
        ),
        out_specs=(
            P(("x", "core"), ("z", "y"), None),
            P(("x", "core"), ("z", "y"), None),
            P(("x", "core", "z", "y"), None),
            P(("x", "core", "z", "y"), None),
            P(("x", "core", "z", "y"), None),
            P(("x", "core", "z", "y"), None),
            P(("z", "y"), ("x", "core")),
            P(("z", "y"), ("x", "core")),
            P(("x", "core"), ("z", "y")),
            P(("x", "core", "z", "y")),
            P(),
            P(),
            P(("x", "core", "z", "y")),
        ),
        check_vma=False,
    )
```
